32 devices in a mesh: dp: 8 (over z, x), fsdp: 4 (over y, core).
Axes of the slice: x: 2, y: 2, z: 4, core: 2. Of those that a mesh axis runs over, the one named last changes fastest.
Arguments:
- tokens: bfloat16 [32, 256, 2048], P(('dp', 'fsdp')), may hold values from -6 to 6
- group_ids: int32 [32], P(('dp', 'fsdp')), may hold values from 0 to 7
- seq_weights: int32 [32], P(('dp', 'fsdp')), may hold values from 1 to 4
- cotangent: bfloat16 [32, 256, 2048], P(('dp', 'fsdp')), may hold values from -6 to 6
- attn_gain: bfloat16 [2048], P(('dp', 'fsdp')), may hold values from 0.5 to 1.5
- w_query: bfloat16 [2048, 2048], P(('dp', 'fsdp')), may hold values from -0.125 to 0.125
- w_key: bfloat16 [2048, 2048], P(('dp', 'fsdp')), may hold values from -0.125 to 0.125
- w_value: bfloat16 [2048, 2048], P(('dp', 'fsdp')), may hold values from -0.125 to 0.125
- w_gate: bfloat16 [2048, 2048], P(('dp', 'fsdp')), may hold values from -0.125 to 0.125
- w_beta: bfloat16 [2048, 16], P(('dp', 'fsdp')), may hold values from -0.125 to 0.125
- conv_query: bfloat16 [4, 2048], P(None, ('dp', 'fsdp')), may hold values from -3 to 3
- conv_key: bfloat16 [4, 2048], P(None, ('dp', 'fsdp')), may hold values from -3 to 3
- conv_value: bfloat16 [4, 2048], P(None, ('dp', 'fsdp')), may hold values from -3 to 3
- head_gain: bfloat16 [128], P(('dp', 'fsdp')), may hold values from 0.5 to 1.5
- w_out: bfloat16 [2048, 2048], P(('dp', 'fsdp')), may hold values from -0.1875 to 0.1875
- mlp_gain: bfloat16 [2048], P(('dp', 'fsdp')), may hold values from 0.5 to 1.5
- w_ffgate: bfloat16 [2048, 5632], P(('dp', 'fsdp')), may hold values from -0.125 to 0.125
- w_ffup: bfloat16 [2048, 5632], P(('dp', 'fsdp')), may hold values from -0.125 to 0.125
- w_ffdown: bfloat16 [5632, 2048], P(('dp', 'fsdp')), may hold values from -0.078125 to 0.078125
Outputs:
- mixed: bfloat16 [32, 256, 2048], P(('dp', 'fsdp'))
- input_grad: float32 [32, 256, 2048], P(('dp', 'fsdp'))
- grad_attn_gain: float32 [2048], P(('dp', 'fsdp'))
- grad_query: float32 [2048, 2048], P(('dp', 'fsdp'))
- grad_key: float32 [2048, 2048], P(('dp', 'fsdp'))
- grad_value: float32 [2048, 2048], P(('dp', 'fsdp'))
- grad_gate: float32 [2048, 2048], P(('dp', 'fsdp'))
- grad_beta: float32 [2048, 16], P(('dp', 'fsdp'))
- grad_conv_query: float32 [4, 2048], P(None, ('dp', 'fsdp'))
- grad_conv_key: float32 [4, 2048], P(None, ('dp', 'fsdp'))
- grad_conv_value: float32 [4, 2048], P(None, ('dp', 'fsdp'))
- grad_head_gain: float32 [128], P(('dp', 'fsdp'))
- grad_out: float32 [2048, 2048], P(('dp', 'fsdp'))
- grad_mlp_gain: float32 [2048], P(('dp', 'fsdp'))
- grad_ffgate: float32 [2048, 5632], P(('dp', 'fsdp'))
- grad_ffup: float32 [2048, 5632], P(('dp', 'fsdp'))
- grad_ffdown: float32 [5632, 2048], P(('dp', 'fsdp'))
The draws below stay inside these ranges and needn't reach their ends.
All inputs are finite; a program needn't handle non-finite values.
Results may differ from the reference program's by a relative error of at most 0.012.
Values may be sent and summed in bfloat16 or wider, within the bound.
No kernel may reach another device: no remote copies, remote signals or barrier semaphores. Data moves between devices by JAX's collectives and lax.ppermute only.
A program may use at most 512 MiB of HBM per device.

```python
import jax
import jax.numpy as jnp
from jax import lax

D = 2048
H = 16
DH = 128
FF = 5632
CONV = 4
BLOCK = 64
GROUPS = 8
SEQ = 256
SEQS = 32


def plant(entries, stream_key, smallest, high):
    longest = entries.shape.index(max(entries.shape))
    spots = []
    for shift in (0, 1):
        where = [jax.random.randint(jax.random.fold_in(stream_key, axis), (), 0, length) for axis, length in enumerate(entries.shape)]
        where[longest] = (where[longest] + shift) % entries.shape[longest]
        spots.append(tuple(where))
    return entries.at[spots[0]].set(smallest).at[spots[1]].set(high)


def steps_of(key, shape, cuts, smallest, top_value):
    def one(dim, shards_of):
        steps = jax.random.uniform(jax.random.fold_in(jax.random.fold_in(key, 6), dim), (shards_of,), jnp.float32, smallest / len(cuts), top_value / len(cuts))
        return jnp.repeat(jnp.exp(steps), shape[dim] // shards_of).reshape((-1,) + (1,) * (len(shape) - dim - 1))

    level = one(*cuts[0])
    for cut in cuts[1:]:
        level = level * one(*cut)
    return level


def noise(rng, dims, width, bound, cuts=(), kind=jnp.bfloat16):
    level = steps_of(rng, dims, cuts, -0.22, 0.18) if cuts else 1.0
    array = jax.random.normal(rng, dims, jnp.float32) * width * level
    return jnp.minimum(jnp.maximum(array, -bound), bound).astype(kind)


def setup_inputs(seed: int = 0) -> dict:
    arg_keys = jax.random.split(jax.random.key(seed), 20)
    return {
        "tokens": noise(arg_keys[0], (SEQS, SEQ, D), 1.0, 6.0, ((0, 32),)),
        "group_ids": plant(jax.random.randint(arg_keys[1], (SEQS,), 0, GROUPS), jax.random.fold_in(arg_keys[1], 1), 0, GROUPS - 1).astype(jnp.int32),
        "seq_weights": plant(jax.random.randint(arg_keys[2], (SEQS,), 1, 5), jax.random.fold_in(arg_keys[2], 1), 1, 4).astype(jnp.int32),
        "cotangent": noise(arg_keys[3], (SEQS, SEQ, D), 1.0, 6.0, ((0, 32),)),
        "attn_gain": jnp.clip(1.0 + 0.1 * jax.random.normal(arg_keys[4], (D,), jnp.float32), 0.5, 1.5).astype(jnp.bfloat16),
        "w_query": noise(arg_keys[5], (D, D), D ** -0.5, 0.125, ((0, 32),)),
        "w_key": noise(arg_keys[6], (D, D), D ** -0.5, 0.125, ((0, 32),)),
        "w_value": noise(arg_keys[7], (D, D), D ** -0.5, 0.125, ((0, 32),)),
        "w_gate": noise(arg_keys[8], (D, D), D ** -0.5, 0.125, ((0, 32),)),
        "w_beta": noise(arg_keys[9], (D, H), D ** -0.5, 0.125, ((0, 32),)),
        "conv_query": noise(arg_keys[10], (CONV, D), CONV ** -0.5, 3.0, ((1, 32),)),
        "conv_key": noise(arg_keys[11], (CONV, D), CONV ** -0.5, 3.0, ((1, 32),)),
        "conv_value": noise(arg_keys[12], (CONV, D), CONV ** -0.5, 3.0, ((1, 32),)),
        "head_gain": jnp.clip(1.0 + 0.1 * jax.random.normal(arg_keys[13], (DH,), jnp.float32), 0.5, 1.5).astype(jnp.bfloat16),
        "w_out": noise(arg_keys[14], (D, D), (D // 2) ** -0.5, 0.1875, ((0, 32),)),
        "mlp_gain": jnp.clip(1.0 + 0.1 * jax.random.normal(arg_keys[15], (D,), jnp.float32), 0.5, 1.5).astype(jnp.bfloat16),
        "w_ffgate": noise(arg_keys[16], (D, FF), D ** -0.5, 0.125, ((0, 32),)),
        "w_ffup": noise(arg_keys[17], (D, FF), D ** -0.5, 0.125, ((0, 32),)),
        "w_ffdown": noise(arg_keys[18], (FF, D), FF ** -0.5, 0.078125, ((0, 32),)),
    }


EPS = 1e-06
HIGHEST = lax.Precision.HIGHEST

@jax.custom_vjp
def low(v):
    return lax.optimization_barrier(v.astype(jnp.bfloat16)).astype(jnp.float32)

@jax.custom_vjp
def low_back(v):
    return v

def low_keep(v):
    return (low(v), None)

def low_pass(kept, grad):
    return (grad,)

def back_keep(v):
    return (v, None)

def back_low(kept, grad):
    return (low(grad),)
low.defvjp(low_keep, low_pass)
low_back.defvjp(back_keep, back_low)

def product(left, right):
    return jnp.dot(left, right, precision=HIGHEST)

def rms_scale(value, gain):
    return value * lax.rsqrt(lax.optimization_barrier(jnp.mean(value * value, axis=-1, keepdims=True)) + EPS) * gain

def short_conv(projected, taps):
    total = taps[0] * projected
    for offset in range(1, taps.shape[0]):
        moved = jnp.pad(projected, ((offset, 0), (0, 0)))[:-offset]
        total = total + taps[offset] * moved
    return jax.nn.silu(total)

def unit_inverse(strict):
    count = strict.shape[-1]
    power = -strict
    result = jnp.eye(count, dtype=strict.dtype) + power
    for repeat in range(count.bit_length() - 2):
        power = jnp.einsum('hij,hjk->hik', power, power, precision=HIGHEST)
        result = result + jnp.einsum('hij,hjk->hik', result, power, precision=HIGHEST)
    return result

def block_step(state, pieces):
    query_blk, key_blk, value_blk, beta_blk = pieces
    count = query_blk.shape[1]
    row_ids = jnp.arange(count)
    strictly = row_ids[:, None] > row_ids[None, :]
    inclusive = row_ids[:, None] >= row_ids[None, :]
    key_beta = key_blk * beta_blk[..., None]
    strict = jnp.where(strictly, jnp.einsum('hcd,hed->hce', key_beta, key_blk, precision=HIGHEST), 0.0)
    inverse = unit_inverse(strict)
    weight_mat = jnp.einsum('hce,hed->hcd', inverse, key_beta, precision=HIGHEST)
    update_mat = jnp.einsum('hce,hed->hcd', inverse, value_blk * beta_blk[..., None], precision=HIGHEST)
    fresh = update_mat - jnp.einsum('hcd,hde->hce', weight_mat, state, precision=HIGHEST)
    scores = jnp.where(inclusive, jnp.einsum('hcd,hed->hce', query_blk, key_blk, precision=HIGHEST), 0.0)
    result = jnp.einsum('hcd,hde->hce', query_blk, state, precision=HIGHEST)
    result = result + jnp.einsum('hce,hev->hcv', scores, fresh, precision=HIGHEST)
    state = state + jnp.einsum('hcd,hcv->hdv', key_blk, fresh, precision=HIGHEST)
    return (state, result)

def delta_rule(query, key, value, beta):
    length, heads, head_size = query.shape
    number = length // BLOCK

    def arrange(item):
        return item.reshape(number, BLOCK, heads, head_size).transpose(0, 2, 1, 3)
    stacked = (arrange(query), arrange(key), arrange(value), beta.reshape(number, BLOCK, heads).transpose(0, 2, 1))
    start = jnp.zeros((heads, head_size, head_size), jnp.float32)
    final, results = lax.scan(jax.checkpoint(block_step), start, stacked)
    return results.transpose(0, 2, 1, 3).reshape(length, heads, head_size)

def mix_heads(query_pre, key_pre, value_pre, gate_pre, beta_pre, conv_query, conv_key, conv_value, head_gain):
    length = query_pre.shape[0]
    heads = beta_pre.shape[1]
    head_size = head_gain.shape[0]

    def split(item):
        return item.reshape(length, heads, head_size)
    query = split(short_conv(query_pre, conv_query))
    query = low(query * lax.rsqrt(lax.optimization_barrier(jnp.sum(query * query, axis=-1, keepdims=True)) + EPS) * head_size ** (-0.5))
    key = split(short_conv(key_pre, conv_key))
    key = low(key * lax.rsqrt(lax.optimization_barrier(jnp.sum(key * key, axis=-1, keepdims=True)) + EPS))
    value = low(split(short_conv(value_pre, conv_value)))
    beta = jax.nn.sigmoid(beta_pre)
    mixer = delta_rule(query, key, value, beta)
    gated = rms_scale(mixer, head_gain) * jax.nn.silu(split(gate_pre))
    return gated.reshape(length, heads * head_size)

def forward_one(inputs, params):
    attn_gain, w_query, w_key, w_value, w_gate, w_beta, conv_query, conv_key, conv_value, head_gain, w_out, mlp_gain, w_ffgate, w_ffup, w_ffdown = params
    normed = low(rms_scale(inputs, attn_gain))
    query_pre = low_back(product(normed, w_query))
    key_pre = low_back(product(normed, w_key))
    value_pre = low_back(product(normed, w_value))
    gate_pre = low_back(product(normed, w_gate))
    beta_pre = low_back(product(normed, w_beta))
    gated = low(mix_heads(query_pre, key_pre, value_pre, gate_pre, beta_pre, conv_query, conv_key, conv_value, head_gain))
    resid = inputs + low_back(product(gated, w_out))
    normed2 = low(rms_scale(resid, mlp_gain))
    gate_ff = low_back(product(normed2, w_ffgate))
    up_ff = low_back(product(normed2, w_ffup))
    hidden = low(jax.nn.silu(gate_ff) * up_ff)
    return resid + low_back(product(hidden, w_ffdown))

def reference(tokens, group_ids, seq_weights, cotangent, attn_gain, w_query, w_key, w_value, w_gate, w_beta, conv_query, conv_key, conv_value, head_gain, w_out, mlp_gain, w_ffgate, w_ffup, w_ffdown):
    params = tuple((item.astype(jnp.float32) for item in (attn_gain, w_query, w_key, w_value, w_gate, w_beta, conv_query, conv_key, conv_value, head_gain, w_out, mlp_gain, w_ffgate, w_ffup, w_ffdown)))
    labels = jnp.arange(GROUPS).astype(jnp.int32)
    hits = group_ids[:, None] == labels[None, :]
    token_count = SEQ * lax.optimization_barrier(jnp.sum(hits.astype(jnp.int32), axis=0))
    own_count = lax.optimization_barrier(jnp.sum(jnp.where(hits, token_count[None, :], 0), axis=1))
    factor = seq_weights.astype(jnp.float32) * (SEQS * SEQ) / (GROUPS * own_count.astype(jnp.float32))

    def one_sequence(carry, item):
        inputs, cotan, scale = item
        final, pullback = jax.vjp(forward_one, inputs.astype(jnp.float32), params)
        d_inputs, d_params = pullback(cotan.astype(jnp.float32) * scale)
        carry = tuple((total + grad for total, grad in zip(carry, d_params)))
        return (carry, (final.astype(jnp.bfloat16), d_inputs))
    zeros = tuple((jnp.zeros_like(item) for item in params))
    grads, (mixed, input_grad) = lax.scan(one_sequence, zeros, (tokens, cotangent, factor))
    return (mixed, input_grad, grads[0], grads[1], grads[2], grads[3], grads[4], grads[5], grads[6], grads[7], grads[8], grads[9], grads[10], grads[11], grads[12], grads[13], grads[14])
```

```python
import functools
import jax
import jax.numpy as jnp
from jax import lax
from jax.experimental import pallas as pl
from jax.experimental.pallas import tpu as pltpu
from jax.sharding import PartitionSpec as P

EPS = 1e-06
BF = jnp.bfloat16
F32 = jnp.float32


def mm(left, right, dims):
    return lax.dot_general(left, right, ((dims[0], dims[1]), ((), ())), preferred_element_type=F32)


NN = ((1,), (0,))
NT = ((1,), (1,))
TN = ((0,), (0,))


def halves(value):
    high = value.astype(BF)
    return high, (value - high.astype(F32)).astype(BF)


def mm3(left, right, dims):
    lh, ll = left
    rh, rl = right
    return mm(lh, rh, dims) + (mm(lh, rl, dims) + mm(ll, rh, dims))


def mm2(left, right, dims):
    lh, ll = left
    return mm(lh, right, dims) + mm(ll, right, dims)


def sigmoid(v):
    return 1.0 / (1.0 + jnp.exp(-v))


def shift_down(v, count, rows):
    if count == 0:
        return v
    return jnp.where(rows >= count, pltpu.roll(v, count, 0), 0.0)


def shift_up(v, count, rows):
    if count == 0:
        return v
    length = v.shape[0]
    return jnp.where(rows < length - count, pltpu.roll(v, length - count, 0), 0.0)


def conv_of(pre, taps, rows):
    total = taps[0] * pre
    for j in range(1, len(taps)):
        total = total + taps[j] * shift_down(pre, j, rows)
    return total


def small_inverse(strict):
    size = strict.shape[0]
    ri = lax.broadcasted_iota(jnp.int32, (size, size), 0)
    ci = lax.broadcasted_iota(jnp.int32, (size, size), 1)
    diff = jnp.bitwise_xor(ri, ci)
    result = jnp.where(ri == ci, 1.0, 0.0) - jnp.where(diff == 1, strict, 0.0)
    span = 2
    while span < size:
        part = jnp.where((diff >= span) & (diff < 2 * span), strict, 0.0)
        rs = halves(result)
        inner = mm3(halves(part), rs, NN)
        result = result - mm3(rs, halves(inner), NN)
        span *= 2
    return result


def head_forward(pre_q, pre_k, pre_v, beta_pre, taps, half):
    length, size = pre_q.shape
    rows = lax.broadcasted_iota(jnp.int32, (length, size), 0)
    cq = conv_of(pre_q, taps[0:4], rows)
    ck = conv_of(pre_k, taps[4:8], rows)
    cv = conv_of(pre_v, taps[8:12], rows)
    sq, sk, sv = sigmoid(cq), sigmoid(ck), sigmoid(cv)
    yq, yk, yv = cq * sq, ck * sk, cv * sv
    rq = lax.rsqrt(jnp.sum(yq * yq, axis=-1, keepdims=True) + EPS)
    rk = lax.rsqrt(jnp.sum(yk * yk, axis=-1, keepdims=True) + EPS)
    query = (yq * rq * size ** (-0.5)).astype(BF)
    key = (yk * rk).astype(BF)
    value = yv.astype(BF)
    beta = sigmoid(beta_pre)
    return (cq, ck, cv, sq, sk, sv, yq, yk, rq, rk, query, key, value, beta, rows)


def lower_masks(length):
    ri = lax.broadcasted_iota(jnp.int32, (length, length), 0)
    ci = lax.broadcasted_iota(jnp.int32, (length, length), 1)
    return ri > ci, ri >= ci


def fwd_kernel(place_ref, pre_ref, bpre_ref, taps_ref, gain_ref, gated_ref, inv_ref, *, heads, size):
    length = pre_ref.shape[0]
    half = length // 2
    width = heads * size
    strictly, inclusive = lower_masks(length)
    for h in range(heads):
        at = pl.ds(h * size, size)
        pre = [pre_ref[:, pl.ds(i * width + h * size, size)] for i in range(4)]
        taps = [taps_ref[i : i + 1, at] for i in range(12)]
        (cq, ck, cv, sq, sk, sv, yq, yk, rq, rk, query, key, value, beta, rows) = head_forward(
            pre[0], pre[1], pre[2], bpre_ref[:, h : h + 1], taps, half
        )
        strict = jnp.where(strictly, mm(key, key, NT) * beta, 0.0)
        top = small_inverse(strict[:half, :half])
        low = small_inverse(strict[half:, half:])
        inv_ref[0, h, 0] = top
        inv_ref[0, h, 1] = low
        rhs = value.astype(F32) * beta
        fresh_top = mm3(halves(top), halves(rhs[:half]), NN)
        ft = halves(fresh_top)
        fresh_low = mm3(
            halves(low), halves(rhs[half:] - mm3(halves(strict[half:, :half]), ft, NN)), NN
        )
        fresh = jnp.concatenate([fresh_top, fresh_low], axis=0)
        scores = jnp.where(inclusive, mm(query, key, NT), 0.0)
        mixer = mm3(halves(scores), halves(fresh), NN)
        scale = lax.rsqrt(jnp.mean(mixer * mixer, axis=-1, keepdims=True) + EPS)
        gate = pre[3]
        gated = mixer * scale * gain_ref[0:1, :] * (gate * sigmoid(gate))
        gated_ref[0, :, at] = gated.astype(BF)


def bwd_kernel(
    place_ref, pre_ref, bpre_ref, taps_ref, gain_ref, inv_ref, dgated_ref,
    dpre_ref, dbeta_ref, dtaps_ref, dgain_ref, *, heads, size,
):
    length = pre_ref.shape[0]
    half = length // 2
    width = heads * size

    @pl.when(pl.program_id(0) == 0)
    def _():
        dtaps_ref[...] = jnp.zeros_like(dtaps_ref)
        dgain_ref[...] = jnp.zeros_like(dgain_ref)

    dbeta_ref[...] = jnp.zeros_like(dbeta_ref)
    strictly, inclusive = lower_masks(length)
    for h in range(heads):
        at = pl.ds(h * size, size)
        pre = [pre_ref[:, pl.ds(i * width + h * size, size)] for i in range(4)]
        taps = [taps_ref[i : i + 1, at] for i in range(12)]
        (cq, ck, cv, sq, sk, sv, yq, yk, rq, rk, query, key, value, beta, rows) = head_forward(
            pre[0], pre[1], pre[2], bpre_ref[:, h : h + 1], taps, half
        )
        gram = mm(key, key, NT)
        strict_low = (gram * beta)[half:, :half]
        top, low = halves(inv_ref[0, h, 0]), halves(inv_ref[0, h, 1])
        cross = halves(strict_low)
        val = value.astype(F32)
        rhs = val * beta
        fresh_top = mm3(top, halves(rhs[:half]), NN)
        fresh_low = mm3(low, halves(rhs[half:] - mm3(cross, halves(fresh_top), NN)), NN)
        fresh = halves(jnp.concatenate([fresh_top, fresh_low], axis=0))
        scores = halves(jnp.where(inclusive, mm(query, key, NT), 0.0))
        mixer = mm3(scores, fresh, NN)
        scale = lax.rsqrt(jnp.mean(mixer * mixer, axis=-1, keepdims=True) + EPS)
        gate = pre[3]
        sg = sigmoid(gate)
        dgated = dgated_ref[0, :, at].astype(F32)
        unit = mixer * scale
        gain = gain_ref[0:1, :]
        dgate = dgated * unit * gain * (sg * (1.0 + gate * (1.0 - sg)))
        dnorm = dgated * (gate * sg)
        dgain_ref[0:1, :] += jnp.sum(dnorm * unit, axis=0, keepdims=True)
        dunit = dnorm * gain
        dmixer = scale * (dunit - unit * jnp.mean(dunit * unit, axis=-1, keepdims=True))
        dm = halves(dmixer)
        dscores = halves(jnp.where(inclusive, mm3(dm, fresh, NT), 0.0))
        dfresh = mm3(scores, dm, TN)
        drhs_low = mm3(low, halves(dfresh[half:]), TN)
        drhs_top = mm3(top, halves(dfresh[:half] - mm3(cross, halves(drhs_low), TN)), TN)
        drhs = jnp.concatenate([drhs_top, drhs_low], axis=0)
        dstrict = jnp.where(strictly, -mm3(halves(drhs), fresh, NT), 0.0)
        dgram = halves(dstrict * beta)
        dquery = mm2(dscores, key, NN)
        dkey = mm2(dscores, query, TN) + mm2(dgram, key, NN) + mm2(dgram, key, TN)
        dval = drhs * beta
        dbeta = jnp.sum(dstrict * gram, axis=-1, keepdims=True) + jnp.sum(
            drhs * val, axis=-1, keepdims=True
        )
        dbeta_ref[:, h : h + 1] = (dbeta * beta * (1.0 - beta)).astype(BF)
        sc = size ** (-0.5)
        uq, uk = yq * rq, yk * rk
        dyq = (rq * sc) * (dquery - uq * jnp.sum(dquery * uq, axis=-1, keepdims=True))
        dyk = rk * (dkey - uk * jnp.sum(dkey * uk, axis=-1, keepdims=True))
        for i, (dy, s, c) in enumerate(((dyq, sq, cq), (dyk, sk, ck), (dval, sv, cv))):
            dc = dy * (s * (1.0 + c * (1.0 - s)))
            total = taps[4 * i] * dc
            for j in range(4):
                dtaps_ref[4 * i + j : 4 * i + j + 1, at] += jnp.sum(
                    dc * shift_down(pre[i], j, rows), axis=0, keepdims=True
                )
                if j:
                    total = total + taps[4 * i + j] * shift_up(dc, j, rows)
            dpre_ref[:, pl.ds(i * width + h * size, size)] = total.astype(BF)
        dpre_ref[:, pl.ds(3 * width + h * size, size)] = dgate.astype(BF)


def delta_forward(place, pre, bpre, taps, gain, slots, heads, size):
    rows = pre.shape[0]
    length = rows // slots
    width = heads * size
    return pl.pallas_call(
        functools.partial(fwd_kernel, heads=heads, size=size),
        grid_spec=pltpu.PrefetchScalarGridSpec(
            num_scalar_prefetch=1,
            grid=(slots,),
            in_specs=[
                pl.BlockSpec((length, 4 * width), lambda i, p: (i, 0)),
                pl.BlockSpec((length, 128), lambda i, p: (i, 0)),
                pl.BlockSpec((16, width), lambda i, p: (0, 0)),
                pl.BlockSpec((8, size), lambda i, p: (0, 0)),
            ],
            out_specs=[
                pl.BlockSpec((1, length, width), lambda i, p: (jnp.bitwise_xor(p[0], i), 0, 0)),
                pl.BlockSpec((1, heads, 2, length // 2, length // 2), lambda i, p: (i, 0, 0, 0, 0)),
            ],
        ),
        out_shape=[
            jax.ShapeDtypeStruct((slots, length, width), BF),
            jax.ShapeDtypeStruct((slots, heads, 2, length // 2, length // 2), F32),
        ],
        compiler_params=pltpu.CompilerParams(vmem_limit_bytes=48 * 1024 * 1024),
        cost_estimate=pl.CostEstimate(
            flops=slots * heads * 400_000_000, bytes_accessed=rows * width * 30, transcendentals=0
        ),
        name="delta_forward",
    )(place, pre, bpre, taps, gain)


def delta_backward(place, pre, bpre, taps, gain, inverse, dgated, slots, heads, size):
    rows = pre.shape[0]
    length = rows // slots
    width = heads * size
    return pl.pallas_call(
        functools.partial(bwd_kernel, heads=heads, size=size),
        grid_spec=pltpu.PrefetchScalarGridSpec(
            num_scalar_prefetch=1,
            grid=(slots,),
            in_specs=[
                pl.BlockSpec((length, 4 * width), lambda i, p: (i, 0)),
                pl.BlockSpec((length, 128), lambda i, p: (i, 0)),
                pl.BlockSpec((16, width), lambda i, p: (0, 0)),
                pl.BlockSpec((8, size), lambda i, p: (0, 0)),
                pl.BlockSpec((1, heads, 2, length // 2, length // 2), lambda i, p: (i, 0, 0, 0, 0)),
                pl.BlockSpec((1, length, width), lambda i, p: (jnp.bitwise_xor(p[0], i), 0, 0)),
            ],
            out_specs=[
                pl.BlockSpec((length, 4 * width), lambda i, p: (i, 0)),
                pl.BlockSpec((length, 128), lambda i, p: (i, 0)),
                pl.BlockSpec((16, width), lambda i, p: (0, 0)),
                pl.BlockSpec((8, size), lambda i, p: (0, 0)),
            ],
        ),
        out_shape=[
            jax.ShapeDtypeStruct((rows, 4 * width), BF),
            jax.ShapeDtypeStruct((rows, 128), BF),
            jax.ShapeDtypeStruct((16, width), F32),
            jax.ShapeDtypeStruct((8, size), F32),
        ],
        compiler_params=pltpu.CompilerParams(vmem_limit_bytes=48 * 1024 * 1024),
        cost_estimate=pl.CostEstimate(
            flops=slots * heads * 800_000_000, bytes_accessed=rows * width * 40, transcendentals=0
        ),
        name="delta_backward",
    )(place, pre, bpre, taps, gain, inverse, dgated)


GROUPS = 8
AXES = ("g", "a", "b", "c")
TEAM = ("a", "b", "c")
SWAP = ((0, 1), (1, 0))
CROSS = ((0, 3), (1, 2), (2, 1), (3, 0))


def swap_a(v):
    return lax.ppermute(v, "a", SWAP)


def swap_b(v):
    return lax.ppermute(v, "b", SWAP)


def swap_c(v):
    return lax.ppermute(v, "c", SWAP)


def team_pieces(v):
    rows = v.shape[0] // 2
    from_a, from_b = swap_a(v), swap_b(v)
    from_ab = jnp.concatenate([swap_b(from_a[:rows]), swap_a(from_b[rows:])], axis=0)
    pieces = []
    for near in (v, from_b, from_a, from_ab):
        pieces += [near, swap_c(near)]
    return pieces


def team_sum(pieces):
    own = []
    for i in range(0, 8, 2):
        own.append(pieces[i] + swap_c(pieces[i + 1].astype(BF)).astype(F32))
    from_b = swap_b(own[1].astype(BF))
    from_a = swap_a(own[2].astype(BF))
    from_ab = lax.ppermute(own[3].astype(BF), ("a", "b"), CROSS)
    return own[0] + from_a.astype(F32) + (from_b.astype(F32) + from_ab.astype(F32))


def team_exchange(v):
    return lax.all_to_all(v, TEAM, 0, 0, tiled=True)


def matmul(left, right):
    return jnp.dot(left, right, preferred_element_type=F32)


def weight_grad(left, right):
    return jnp.einsum("ra,rb->ab", left, right, preferred_element_type=F32)


def back_grad(grad, weight):
    return jnp.einsum("rb,ab->ra", grad, weight, preferred_element_type=F32)


def rms_unit(value):
    scale = lax.rsqrt(jnp.mean(value * value, axis=-1, keepdims=True) + EPS)
    return value * scale, scale


def rms_pull(unit, scale, gain, grad):
    inner = grad * gain
    return scale * (inner - unit * jnp.mean(inner * unit, axis=-1, keepdims=True))


def gather_small(v, groups):
    index = [lax.axis_index(k) for k in AXES]
    both = v[None]
    for axis, swap in (("c", swap_c), ("b", swap_b), ("a", swap_a)):
        other = swap(both)
        mine = lax.axis_index(axis) == 0
        both = jnp.concatenate(
            [jnp.where(mine, both, other), jnp.where(mine, other, both)], axis=0
        )
    whole = jnp.zeros((groups,) + both.shape, both.dtype)
    whole = lax.dynamic_update_index_in_dim(whole, both, index[0], 0)
    for step in range(1, groups):
        got = lax.ppermute(both, "g", [(j, (j + step) % groups) for j in range(groups)])
        whole = lax.dynamic_update_index_in_dim(whole, got, (index[0] - step) % groups, 0)
    return whole.reshape(-1, v.shape[0])


def group_sum_small(v, groups):
    me = lax.axis_index("g")
    total = lax.dynamic_index_in_dim(v, me, 0, False)
    for step in range(1, groups):
        send = lax.dynamic_index_in_dim(v, (me + step) % groups, 0, False)
        total = total + lax.ppermute(send, "g", [(j, (j + step) % groups) for j in range(groups)])
    return total


def group_scatter(v):
    return lax.psum_scatter(v, "g", scatter_dimension=0, tiled=True)


def on_device(
    tokens, group_ids, seq_weights, cotangent, attn_gain, w_query, w_key, w_value, w_gate, w_beta,
    conv_query, conv_key, conv_value, head_gain, w_out, mlp_gain, w_ffgate, w_ffup, w_ffdown,
):
    groups = lax.axis_size("g")
    team = 8
    devices = groups * team
    seqs, length, width = tokens.shape
    span = attn_gain.shape[0]
    taps = conv_query.shape[0]
    heads = w_beta.shape[1]
    size = head_gain.shape[0] * devices
    ff = w_ffgate.shape[1]
    cols = width // team
    own_heads = heads // team
    ff_rows = w_ffdown.shape[0]
    ff_cols = groups * ff_rows
    member = lax.axis_index(TEAM)
    group = lax.axis_index("g")

    mixer_w = jnp.concatenate(
        [w.reshape(span, team, cols) for w in (w_query, w_key, w_value, w_gate)], axis=2
    ).transpose(1, 0, 2)
    mixer_w = team_exchange(mixer_w).reshape(team * span, 4 * cols)
    mixer_w = lax.all_gather(mixer_w, "g", axis=0, tiled=True)

    x_own = tokens.reshape(length, width)
    x_pieces = team_pieces(x_own)

    small = jnp.concatenate(
        [
            attn_gain, mlp_gain,
            conv_query.reshape(-1), conv_key.reshape(-1), conv_value.reshape(-1),
            head_gain, w_beta.reshape(-1),
            group_ids.astype(BF), seq_weights.astype(BF),
        ]
    )
    small = jnp.pad(small, (0, -small.shape[0] % 128))
    small = gather_small(small, groups)
    at = 0

    def take(count):
        nonlocal at
        part = small[:, at : at + count]
        at += count
        return part

    gain_one = take(span).reshape(-1).astype(F32)
    gain_two = take(span).reshape(-1).astype(F32)
    all_taps = [
        take(taps * span).reshape(devices, taps, span).transpose(1, 0, 2).reshape(taps, width)
        for _ in range(3)
    ]
    gain_head = take(head_gain.shape[0]).reshape(-1).astype(F32)
    beta_w = take(span * heads).reshape(width, heads)
    ids = take(1).reshape(-1)
    factor_w = take(1).reshape(-1)
    own_taps = lax.dynamic_slice_in_dim(
        jnp.concatenate(all_taps, axis=0).astype(F32), member * cols, cols, 1
    )
    own_taps = jnp.pad(own_taps, ((0, 16 - 3 * taps), (0, 0)))
    head_rows = jnp.pad(gain_head[None], ((0, 7), (0, 0)))
    beta_w = jnp.pad(
        lax.dynamic_slice_in_dim(beta_w, member * own_heads, own_heads, 1),
        ((0, 0), (0, 128 - own_heads)),
    )
    own_id = group_ids.astype(F32)[0]
    count = jnp.sum((ids.astype(F32) == own_id).astype(jnp.int32)) * length
    factor = (
        seq_weights.astype(F32)[0] * (devices * seqs * length) / (GROUPS * count.astype(F32))
    )

    d_final = cotangent.reshape(length, width).astype(F32) * factor
    d_down = jnp.concatenate(team_pieces(d_final.astype(BF)), axis=0)

    out_w = lax.all_gather(w_out, "g", axis=0, tiled=False)
    ff_w = jnp.concatenate(
        [
            w.reshape(span, groups, team, ff_rows).transpose(2, 0, 1, 3).reshape(team, span, ff_cols)
            for w in (w_ffgate, w_ffup)
        ],
        axis=2,
    )
    ff_w = team_exchange(ff_w).reshape(team * span, 2 * ff_cols)
    ff_w = lax.all_gather(ff_w, "g", axis=0, tiled=True)
    down_w = lax.all_gather(w_ffdown, "g", axis=0, tiled=True)
    out_full = jnp.zeros((groups, team, span, width), BF)
    for i, piece in enumerate(team_pieces(out_w.reshape(groups * span, width))):
        out_full = lax.dynamic_update_slice(
            out_full,
            piece.reshape(groups, 1, span, width),
            (0, jnp.bitwise_xor(member, i), 0, 0),
        )
    out_full = out_full.reshape(width, width)

    normed = jnp.concatenate(
        [(rms_unit(p.astype(F32))[0] * gain_one).astype(BF) for p in x_pieces], axis=0
    )
    beta_pre = matmul(normed, beta_w)
    pre = matmul(normed, mixer_w)
    place = member.astype(jnp.int32).reshape(1)
    gated, inverse = delta_forward(
        place, pre, beta_pre, own_taps, head_rows, team, own_heads, size
    )
    gated = team_exchange(gated).transpose(1, 0, 2).reshape(length, width)
    inputs = x_own.astype(F32)
    resid = inputs + matmul(gated, out_full)

    unit_two, scale_two = rms_unit(resid)
    normed_two = jnp.concatenate(team_pieces((unit_two * gain_two).astype(BF)), axis=0)
    gate_w, up_w = ff_w[:, :ff_cols], ff_w[:, ff_cols:]
    gate_ff = matmul(normed_two, gate_w)
    up_ff = matmul(normed_two, up_w)
    d_hidden = back_grad(d_down, down_w)
    sig = jax.nn.sigmoid(gate_ff)
    silu = gate_ff * sig
    hidden = (silu * up_ff).astype(BF)
    d_gate = (d_hidden * up_ff * (sig + silu * (1.0 - sig))).astype(BF)
    d_up = (d_hidden * silu).astype(BF)
    d_normed_two = back_grad(d_gate, gate_w) + back_grad(d_up, up_w)

    def split(v):
        return [v[i * length : (i + 1) * length] for i in range(team)]

    d_normed_two = team_sum(split(d_normed_two))
    final = resid + team_sum(split(matmul(hidden, down_w)))
    mixed = final.astype(BF).reshape(seqs, length, width)
    grad_ffdown = group_scatter(weight_grad(hidden, d_down).astype(BF)).astype(F32)

    def ff_home(v):
        v = group_scatter(v.astype(BF))
        v = team_exchange(v).reshape(team, span, groups, ff_rows)
        return v.transpose(1, 2, 0, 3).reshape(span, ff).astype(F32)

    grad_ffgate = ff_home(weight_grad(normed_two, d_gate))
    grad_ffup = ff_home(weight_grad(normed_two, d_up))
    mlp_part = jnp.sum(d_normed_two * unit_two, axis=0)
    d_resid = d_final + rms_pull(unit_two, scale_two, gain_two, d_normed_two)

    d_branch = d_resid.astype(BF)
    d_gated = back_grad(d_branch, out_full).astype(BF)
    d_gated = team_exchange(
        d_gated.reshape(length, team, cols).transpose(1, 0, 2)
    )
    gated_rows = gated.reshape(length, groups, team, span)
    grad_out = []
    for i in range(team):
        part = lax.dynamic_index_in_dim(gated_rows, jnp.bitwise_xor(member, i), 2, False)
        grad_out.append(weight_grad(part.reshape(length, groups * span), d_branch))
    grad_out = group_scatter(team_sum(grad_out).astype(BF)).astype(F32)
    d_pre, d_beta, d_taps, d_head = delta_backward(
        place, pre, beta_pre, own_taps, head_rows, inverse, d_gated, team, own_heads, size
    )
    grads = weight_grad(normed, d_pre)
    grad_beta = weight_grad(normed, d_beta)[:, :own_heads]
    d_normed = back_grad(d_pre, mixer_w) + back_grad(d_beta, beta_w)
    x_units = jnp.concatenate([rms_unit(p.astype(F32))[0] for p in x_pieces], axis=0)
    attn_part = jnp.sum(d_normed * x_units, axis=0)
    mixer_grads = team_exchange(group_scatter(grads.astype(BF)))
    mixer_grads = mixer_grads.reshape(team, span, 4, cols).transpose(2, 1, 0, 3)
    mixer_grads = mixer_grads.reshape(4, span, width).astype(F32)

    tap_rows = lax.dynamic_update_slice_in_dim(
        jnp.zeros((3 * taps, width), F32), d_taps[: 3 * taps], member * cols, 1
    )
    head_part = jnp.pad(
        d_head[0].reshape(devices, -1), ((0, 0), (0, span - head_gain.shape[0]))
    )
    extra = jnp.concatenate(
        [
            grad_beta, attn_part[:, None], tap_rows.T, head_part.reshape(-1)[:, None],
            mlp_part[:, None],
        ],
        axis=1,
    )
    kinds = extra.shape[1]
    extra = extra.reshape(groups, team, span * kinds)
    extra = jnp.pad(extra, ((0, 0), (0, 0), (0, -extra.shape[2] % 128)))
    extra = team_exchange(group_sum_small(extra, groups))
    extra = extra[:, : span * kinds].reshape(team, span, kinds)
    grad_beta = extra[:, :, :own_heads].transpose(1, 0, 2).reshape(span, heads)
    rest = jnp.sum(extra[:, :, own_heads:], axis=0)
    grad_attn = rest[:, 0]
    grad_taps = rest[:, 1 : 1 + 3 * taps].T.reshape(3, taps, span)
    grad_head = rest[: head_gain.shape[0], 1 + 3 * taps]
    grad_mlp = rest[:, 2 + 3 * taps]

    d_normed = team_sum(split(d_normed))
    unit_one, scale_one = rms_unit(inputs)
    input_grad = d_resid + rms_pull(unit_one, scale_one, gain_one, d_normed)
    return (
        mixed,
        input_grad.reshape(seqs, length, width),
        grad_attn,
        mixer_grads[0],
        mixer_grads[1],
        mixer_grads[2],
        mixer_grads[3],
        grad_beta,
        grad_taps[0],
        grad_taps[1],
        grad_taps[2],
        grad_head,
        grad_out,
        grad_mlp,
        grad_ffgate,
        grad_ffup,
        grad_ffdown,
    )


def solution(mesh):
    dp, fsdp = mesh.shape["dp"], mesh.shape["fsdp"]
    finer = jax.sharding.Mesh(mesh.devices.reshape(dp // 2, 2, fsdp // 2, 2), AXES)
    one, rows, last = P(AXES), P(AXES, None), P(None, AXES)
    seq = P(AXES, None, None)
    return jax.shard_map(
        on_device,
        mesh=finer,
        in_specs=(
            seq, one, one, seq, one, rows, rows, rows, rows, rows, last, last, last, one, rows,
            one, rows, rows, rows,
        ),
        out_specs=(
            seq, seq, one, rows, rows, rows, rows, rows, last, last, last, one, rows, one, rows,
            rows, rows,
        ),
        check_vma=False,
    )
```

```python
import collections
import functools
import jax
import jax.numpy as jnp
from jax import lax
from jax.experimental import pallas as pl
from jax.experimental.pallas import tpu as pltpu
from jax.sharding import PartitionSpec as P

EPS = 1e-06
BF = jnp.bfloat16
F32 = jnp.float32


def mm(left, right, dims):
    return lax.dot_general(left, right, ((dims[0], dims[1]), ((), ())), preferred_element_type=F32)


NN = ((1,), (0,))
NT = ((1,), (1,))
TN = ((0,), (0,))


def halves(value):
    high = value.astype(BF)
    return high, (value - high.astype(F32)).astype(BF)


def mm3(left, right, dims):
    lh, ll = left
    rh, rl = right
    return mm(lh, rh, dims) + (mm(lh, rl, dims) + mm(ll, rh, dims))


def mm2(left, right, dims):
    lh, ll = left
    return mm(lh, right, dims) + mm(ll, right, dims)


def sigmoid(v):
    return 1.0 / (1.0 + jnp.exp(-v))


def shift_down(v, count, rows):
    if count == 0:
        return v
    return jnp.where(rows >= count, pltpu.roll(v, count, 0), 0.0)


def shift_up(v, count, rows):
    if count == 0:
        return v
    length = v.shape[0]
    return jnp.where(rows < length - count, pltpu.roll(v, length - count, 0), 0.0)


def conv_of(pre, taps, rows):
    total = taps[0] * pre
    for j in range(1, len(taps)):
        total = total + taps[j] * shift_down(pre, j, rows)
    return total


def unit_inverses(stricts):
    size = stricts[0].shape[0]
    ri = lax.broadcasted_iota(jnp.int32, (size, size), 0)
    ci = lax.broadcasted_iota(jnp.int32, (size, size), 1)
    diff = jnp.bitwise_xor(ri, ci)
    eye = jnp.where(ri == ci, 1.0, 0.0)
    results = [eye - jnp.where(diff == 1, strict, 0.0) for strict in stricts]
    span = 2
    while span < size:
        here = (diff >= span) & (diff < 2 * span)
        split = [halves(result) for result in results]
        inner = [mm3(halves(jnp.where(here, s, 0.0)), r, NN) for s, r in zip(stricts, split)]
        inner = [halves(i) for i in inner]
        results = [t - mm3(r, i, NN) for t, r, i in zip(results, split, inner)]
        span *= 2
    return results


def head_forward(pre_q, pre_k, pre_v, beta_pre, taps):
    length, size = pre_q.shape
    rows = lax.broadcasted_iota(jnp.int32, (length, size), 0)
    cq = conv_of(pre_q, taps[0:4], rows)
    ck = conv_of(pre_k, taps[4:8], rows)
    cv = conv_of(pre_v, taps[8:12], rows)
    sq, sk, sv = sigmoid(cq), sigmoid(ck), sigmoid(cv)
    yq, yk, yv = cq * sq, ck * sk, cv * sv
    rq = lax.rsqrt(jnp.sum(yq * yq, axis=-1, keepdims=True) + EPS)
    rk = lax.rsqrt(jnp.sum(yk * yk, axis=-1, keepdims=True) + EPS)
    query = (yq * rq * size ** (-0.5)).astype(BF)
    key = (yk * rk).astype(BF)
    value = yv.astype(BF)
    beta = sigmoid(beta_pre)
    return (cq, ck, cv, sq, sk, sv, yq, yk, rq, rk, query, key, value, beta, rows)


def lower_masks(length):
    ri = lax.broadcasted_iota(jnp.int32, (length, length), 0)
    ci = lax.broadcasted_iota(jnp.int32, (length, length), 1)
    return ri > ci, ri >= ci


def fwd_kernel(
    place_ref, pre_ref, bpre_ref, taps_ref, gain_ref, gated_ref, inv_ref, *, heads, size, length
):
    half = length // 2
    width = heads * size
    flip = place_ref[0] & (gated_ref.shape[0] - 1)
    strictly, inclusive = lower_masks(length)
    work = []
    blocks = []
    chains = [(b, h) for b in range(pre_ref.shape[0] // length) for h in range(heads)]
    for b, h in chains:
        at = pl.ds(h * size, size)
        rows = pl.ds(b * length, length)
        pre = [pre_ref[rows, pl.ds(i * width + h * size, size)] for i in range(3)]
        taps = [taps_ref[i : i + 1, at] for i in range(12)]
        made = head_forward(*pre, bpre_ref[rows, h : h + 1], taps)
        query, key, value, beta = made[10:14]
        strict = jnp.where(strictly, mm(key, key, NT) * beta, 0.0)
        blocks += [strict[:half, :half], strict[half:, half:]]
        scores = jnp.where(inclusive, mm(query, key, NT), 0.0)
        work.append((halves(strict[half:, :half]), value.astype(F32) * beta, halves(scores)))
    inverses = unit_inverses(blocks)
    for n, (b, h) in enumerate(chains):
        inv_ref[b, h, 0] = inverses[2 * n]
        inv_ref[b, h, 1] = inverses[2 * n + 1]
    tops = [mm3(halves(inverses[2 * n]), halves(w[1][:half]), NN) for n, w in enumerate(work)]
    lows = [w[1][half:] - mm3(w[0], halves(top), NN) for w, top in zip(work, tops)]
    lows = [mm3(halves(inverses[2 * n + 1]), halves(low), NN) for n, low in enumerate(lows)]
    mixers = [
        mm3(w[2], halves(jnp.concatenate([top, low], axis=0)), NN)
        for w, top, low in zip(work, tops, lows)
    ]
    for (b, h), mixer in zip(chains, mixers):
        at = pl.ds(h * size, size)
        rows = pl.ds(b * length, length)
        scale = lax.rsqrt(jnp.mean(mixer * mixer, axis=-1, keepdims=True) + EPS)
        gate = pre_ref[rows, pl.ds(3 * width + h * size, size)]
        gated = mixer * scale * gain_ref[0:1, :] * (gate * sigmoid(gate))
        gated_ref[b ^ flip, :, at] = gated.astype(BF)


def bwd_chain(refs, b, h, heads, size, length, masks, sums):
    pre_ref, bpre_ref, taps_ref, gain_ref, inv_ref, dgated_ref, dpre_ref, dbeta_ref, flip = refs
    strictly, inclusive = masks
    half = length // 2
    width = heads * size
    at = pl.ds(h * size, size)
    line = pl.ds(b * length, length)
    cols = [pl.ds(i * width + h * size, size) for i in range(4)]
    taps = [taps_ref[i : i + 1, at] for i in range(12)]
    made = head_forward(
        *[pre_ref[line, c] for c in cols[:3]], bpre_ref[line, h : h + 1], taps
    )
    (cq, ck, cv, sq, sk, sv, yq, yk, rq, rk, query, key, value, beta, rows) = made
    yield
    gram = mm(key, key, NT)
    cross = halves((gram * beta)[half:, :half])
    scores = halves(jnp.where(inclusive, mm(query, key, NT), 0.0))
    top, low = halves(inv_ref[b, h, 0]), halves(inv_ref[b, h, 1])
    val = value.astype(F32)
    rhs = val * beta
    yield
    fresh_top = mm3(top, halves(rhs[:half]), NN)
    yield
    fresh_low = rhs[half:] - mm3(cross, halves(fresh_top), NN)
    yield
    fresh_low = mm3(low, halves(fresh_low), NN)
    fresh = halves(jnp.concatenate([fresh_top, fresh_low], axis=0))
    yield
    mixer = mm3(scores, fresh, NN)
    yield
    scale = lax.rsqrt(jnp.mean(mixer * mixer, axis=-1, keepdims=True) + EPS)
    gate = pre_ref[line, cols[3]]
    sg = sigmoid(gate)
    dgated = dgated_ref[b ^ flip, :, at].astype(F32)
    unit = mixer * scale
    gain = gain_ref[0:1, :]
    dgate = dgated * unit * gain * (sg * (1.0 + gate * (1.0 - sg)))
    dnorm = dgated * (gate * sg)
    sums["gain"].append(jnp.sum(dnorm * unit, axis=0, keepdims=True))
    dunit = dnorm * gain
    dmixer = scale * (dunit - unit * jnp.mean(dunit * unit, axis=-1, keepdims=True))
    dm = halves(dmixer)
    dpre_ref[line, cols[3]] = dgate.astype(BF)
    yield
    dscores = halves(jnp.where(inclusive, mm3(dm, fresh, NT), 0.0))
    dfresh = mm3(scores, dm, TN)
    yield
    drhs_low = mm3(low, halves(dfresh[half:]), TN)
    yield
    drhs_top = dfresh[:half] - mm3(cross, halves(drhs_low), TN)
    yield
    drhs_top = mm3(top, halves(drhs_top), TN)
    drhs = jnp.concatenate([drhs_top, drhs_low], axis=0)
    yield
    dstrict = jnp.where(strictly, -mm3(halves(drhs), fresh, NT), 0.0)
    dgram = halves(dstrict * beta)
    dval = drhs * beta
    dbeta = jnp.sum(dstrict * gram, axis=-1, keepdims=True) + jnp.sum(
        drhs * val, axis=-1, keepdims=True
    )
    dbeta_ref[line, h : h + 1] = (dbeta * beta * (1.0 - beta)).astype(BF)
    yield
    dquery = mm2(dscores, key, NN)
    dkey = mm2(dscores, query, TN) + mm2(dgram, key, NN) + mm2(dgram, key, TN)
    yield
    sc = size ** (-0.5)
    uq, uk = yq * rq, yk * rk
    dyq = (rq * sc) * (dquery - uq * jnp.sum(dquery * uq, axis=-1, keepdims=True))
    dyk = rk * (dkey - uk * jnp.sum(dkey * uk, axis=-1, keepdims=True))
    for i, (dy, s, c) in enumerate(((dyq, sq, cq), (dyk, sk, ck), (dval, sv, cv))):
        dc = dy * (s * (1.0 + c * (1.0 - s)))
        total = taps[4 * i] * dc
        for j in range(4):
            moved = shift_down(pre_ref[line, cols[i]], j, rows)
            sums[4 * i + j, h].append(jnp.sum(dc * moved, axis=0, keepdims=True))
            if j:
                total = total + taps[4 * i + j] * shift_up(dc, j, rows)
        dpre_ref[line, cols[i]] = total.astype(BF)
        yield


def bwd_kernel(
    place_ref, pre_ref, bpre_ref, taps_ref, gain_ref, inv_ref, dgated_ref,
    dpre_ref, dbeta_ref, dtaps_ref, dgain_ref, *, heads, size, length,
):
    @pl.when(pl.program_id(0) == 0)
    def _():
        dtaps_ref[...] = jnp.zeros_like(dtaps_ref)
        dgain_ref[...] = jnp.zeros_like(dgain_ref)

    dbeta_ref[...] = jnp.zeros_like(dbeta_ref)
    masks = lower_masks(length)
    sums = collections.defaultdict(list)
    flip = place_ref[0] & (dgated_ref.shape[0] - 1)
    refs = (
        pre_ref, bpre_ref, taps_ref, gain_ref, inv_ref, dgated_ref, dpre_ref, dbeta_ref, flip
    )
    chains = [
        bwd_chain(refs, b, h, heads, size, length, masks, sums)
        for b in range(dgated_ref.shape[0])
        for h in range(heads)
    ]
    while chains:
        chains = [chain for chain in chains if next(chain, True) is None]
    dgain_ref[0:1, :] += sum(sums.pop("gain"))
    for (row, h), parts in sums.items():
        dtaps_ref[row : row + 1, pl.ds(h * size, size)] += sum(parts)


PAIR = 2


def team_block(i, p):
    return (jnp.bitwise_xor(p[0] // PAIR, i), 0, 0)


def delta_forward(place, pre, bpre, taps, gain, slots, heads, size):
    rows = pre.shape[0]
    length = rows // slots
    width = heads * size
    return pl.pallas_call(
        functools.partial(fwd_kernel, heads=heads, size=size, length=length),
        grid_spec=pltpu.PrefetchScalarGridSpec(
            num_scalar_prefetch=1,
            grid=(slots // PAIR,),
            in_specs=[
                pl.BlockSpec((PAIR * length, 4 * width), lambda i, p: (i, 0)),
                pl.BlockSpec((PAIR * length, 128), lambda i, p: (i, 0)),
                pl.BlockSpec((16, width), lambda i, p: (0, 0)),
                pl.BlockSpec((8, size), lambda i, p: (0, 0)),
            ],
            out_specs=[
                pl.BlockSpec((PAIR, length, width), team_block),
                pl.BlockSpec((PAIR, heads, 2, length // 2, length // 2), lambda i, p: (i, 0, 0, 0, 0)),
            ],
        ),
        out_shape=[
            jax.ShapeDtypeStruct((slots, length, width), BF),
            jax.ShapeDtypeStruct((slots, heads, 2, length // 2, length // 2), F32),
        ],
        compiler_params=pltpu.CompilerParams(vmem_limit_bytes=48 * 1024 * 1024),
        cost_estimate=pl.CostEstimate(
            flops=slots * heads * 100_000_000, bytes_accessed=rows * width * 4, transcendentals=0
        ),
        name="delta_forward",
    )(place, pre, bpre, taps, gain)


def delta_backward(place, pre, bpre, taps, gain, inverse, dgated, slots, heads, size):
    rows = pre.shape[0]
    length = rows // slots
    width = heads * size
    return pl.pallas_call(
        functools.partial(bwd_kernel, heads=heads, size=size, length=length),
        grid_spec=pltpu.PrefetchScalarGridSpec(
            num_scalar_prefetch=1,
            grid=(slots // PAIR,),
            in_specs=[
                pl.BlockSpec((PAIR * length, 4 * width), lambda i, p: (i, 0)),
                pl.BlockSpec((PAIR * length, 128), lambda i, p: (i, 0)),
                pl.BlockSpec((16, width), lambda i, p: (0, 0)),
                pl.BlockSpec((8, size), lambda i, p: (0, 0)),
                pl.BlockSpec((PAIR, heads, 2, length // 2, length // 2), lambda i, p: (i, 0, 0, 0, 0)),
                pl.BlockSpec((PAIR, length, width), team_block),
            ],
            out_specs=[
                pl.BlockSpec((PAIR * length, 4 * width), lambda i, p: (i, 0)),
                pl.BlockSpec((PAIR * length, 128), lambda i, p: (i, 0)),
                pl.BlockSpec((16, width), lambda i, p: (0, 0)),
                pl.BlockSpec((8, size), lambda i, p: (0, 0)),
            ],
        ),
        out_shape=[
            jax.ShapeDtypeStruct((rows, 4 * width), BF),
            jax.ShapeDtypeStruct((rows, 128), BF),
            jax.ShapeDtypeStruct((16, width), F32),
            jax.ShapeDtypeStruct((8, size), F32),
        ],
        compiler_params=pltpu.CompilerParams(vmem_limit_bytes=48 * 1024 * 1024),
        cost_estimate=pl.CostEstimate(
            flops=slots * heads * 100_000_000, bytes_accessed=rows * width * 4, transcendentals=0
        ),
        name="delta_backward",
    )(place, pre, bpre, taps, gain, inverse, dgated)


def load_piece(step, pieces, buf, sem):
    def start(which):
        for n, piece in enumerate(pieces):

            @pl.when(which == n)
            def _():
                pltpu.make_async_copy(piece, buf.at[n % 2], sem.at[n % 2]).start()

    @pl.when(step == 0)
    def _():
        start(0)

    start(step + 1)
    slot = lax.rem(step, 2)
    pltpu.make_async_copy(pieces[0], buf.at[slot], sem.at[slot]).wait()
    return buf[slot]


def piece_scratch(piece):
    return [pltpu.VMEM((2,) + piece.shape, piece.dtype), pltpu.SemaphoreType.DMA((2,))]


ANY = pl.BlockSpec(memory_space=pl.ANY)


def assemble_kernel(place_ref, *refs):
    *pieces, out_ref, buf, sem = refs
    out_ref[:, 0] = load_piece(pl.program_id(0), pieces, buf, sem)


def assemble(place, pieces):
    groups, rows, width = pieces[0].shape
    count = len(pieces)
    return pl.pallas_call(
        assemble_kernel,
        grid_spec=pltpu.PrefetchScalarGridSpec(
            num_scalar_prefetch=1,
            grid=(count,),
            in_specs=[ANY] * count,
            out_specs=pl.BlockSpec(
                (groups, 1, rows, width), lambda i, p: (0, jnp.bitwise_xor(p[0], i), 0, 0)
            ),
            scratch_shapes=piece_scratch(pieces[0]),
        ),
        out_shape=jax.ShapeDtypeStruct((groups, count, rows, width), BF),
        cost_estimate=pl.CostEstimate(
            flops=0, bytes_accessed=4 * count * groups * rows * width, transcendentals=0
        ),
        name="assemble",
    )(place, *pieces)


def ff_tile(n, d, gu_ref, down_ref, hid_ref, dgu_ref):
    cols = hid_ref.shape[1]
    main = cols // 128 * 128
    gu_w = gu_ref[...]
    gu = mm(n, gu_w, NN)
    dh = mm(d, down_ref[...], NT)
    spans = [(0, main, main, 0)]
    if main < cols:
        spans.append((2 * main, main + cols, cols - main, main))
    for gate_at, up_at, count, at in spans:
        gate, up = gu[:, gate_at : gate_at + count], gu[:, up_at : up_at + count]
        grad = dh[:, at : at + count]
        sig = sigmoid(gate)
        silu = gate * sig
        hid_ref[:, at : at + count] = (silu * up).astype(BF)
        dgu_ref[:, gate_at : gate_at + count] = (grad * up * (sig + silu * (1.0 - sig))).astype(BF)
        dgu_ref[:, up_at : up_at + count] = (grad * silu).astype(BF)
    return mm(dgu_ref[...], gu_w, NT), mm(hid_ref[...], down_ref[...], NN)


def ff_first_kernel(gu_ref, down_ref, *refs):
    ns, ds = refs[:8], refs[8:16]
    n_ref, d_ref, hid_ref, dgu_ref, dn_ref, out_ref, n_buf, n_sem, d_buf, d_sem = refs[16:]
    step = pl.program_id(0)
    n = load_piece(step, ns, n_buf, n_sem)
    d = load_piece(step, ds, d_buf, d_sem)
    n_ref[...] = n
    d_ref[...] = d
    dn, out = ff_tile(n, d, gu_ref, down_ref, hid_ref, dgu_ref)
    dn_ref[...] = dn.astype(BF)
    out_ref[...] = out.astype(BF)


def put_pair(step, value, even_ref, odd_ref):
    value = value.astype(BF)

    @pl.when(lax.rem(step, 2) == 0)
    def _():
        even_ref[...] = value

    @pl.when(lax.rem(step, 2) == 1)
    def _():
        odd_ref[...] = value


def ff_more_kernel(
    gu_ref, down_ref, n_ref, d_ref, dn_in, out_in,
    hid_ref, dgu_ref, dn_even, dn_odd, out_even, out_odd,
):
    dn, out = ff_tile(n_ref[...], d_ref[...], gu_ref, down_ref, hid_ref, dgu_ref)
    step = pl.program_id(0)
    put_pair(step, dn + dn_in[...].astype(F32), dn_even, dn_odd)
    put_pair(step, out + out_in[...].astype(F32), out_even, out_odd)


def feed_forward(gu, down, ns=None, ds=None, more=None):
    cols, width = down.shape
    tile = ns[0].shape[0] if more is None else more[0].shape[0] // 8
    rows = 8 * tile

    def row(count):
        return pl.BlockSpec((tile, count), lambda i: (i, 0))

    pair = pl.BlockSpec((tile, width), lambda i: (i // 2, 0))
    if more is None:
        outs = [width, width, cols, 2 * cols, width, width]
        out_specs = [row(k) for k in outs]
        shapes = [(rows, k) for k in outs]
    else:
        out_specs = [row(cols), row(2 * cols)] + [pair] * 4
        shapes = [(rows, cols), (rows, 2 * cols)] + [(rows // 2, width)] * 4
    return pl.pallas_call(
        ff_first_kernel if more is None else ff_more_kernel,
        grid=(8,),
        in_specs=[
            pl.BlockSpec((width, 2 * cols), lambda i: (0, 0)),
            pl.BlockSpec((cols, width), lambda i: (0, 0)),
        ]
        + ([ANY] * 16 if more is None else [row(width)] * 4),
        out_specs=out_specs,
        out_shape=[jax.ShapeDtypeStruct(k, BF) for k in shapes],
        scratch_shapes=piece_scratch(ns[0]) + piece_scratch(ds[0]) if more is None else [],
        compiler_params=pltpu.CompilerParams(vmem_limit_bytes=56 * 1024 * 1024),
        cost_estimate=pl.CostEstimate(
            flops=rows * width * cols, bytes_accessed=2 * rows * width, transcendentals=0
        ),
        name="feed_forward",
    )(gu, down, *(tuple(ns) + tuple(ds) if more is None else more))


def pull_kernel(dpre_ref, dbeta_ref, w_ref, beta_ref, *refs):
    even_ref, odd_ref, part_ref, buf, sem = refs[8:]

    @pl.when(pl.program_id(0) == 0)
    def _():
        part_ref[...] = jnp.zeros_like(part_ref)

    x = load_piece(pl.program_id(0), refs[:8], buf, sem).astype(F32)
    unit = x * lax.rsqrt(jnp.mean(x * x, axis=-1, keepdims=True) + EPS)
    w = w_ref[...].reshape(-1, w_ref.shape[-1])
    dn = mm(dpre_ref[...], w, NT) + mm(dbeta_ref[...], beta_ref[...], NT)
    part_ref[...] += jnp.sum((dn * unit).reshape(-1, 8, dn.shape[1]), axis=0)
    put_pair(pl.program_id(0), dn, even_ref, odd_ref)


def pull_projections(dpre, dbeta, x, w, beta_w):
    tile, width = x[0].shape
    rows, cols = dpre.shape
    groups = w.shape[0]

    def row(count):
        return pl.BlockSpec((tile, count), lambda i: (i, 0))

    return pl.pallas_call(
        pull_kernel,
        grid=(rows // tile,),
        in_specs=[
            row(cols),
            row(dbeta.shape[1]),
            pl.BlockSpec((groups, width // groups, cols), lambda i: (0, 0, 0)),
            pl.BlockSpec(beta_w.shape, lambda i: (0, 0)),
        ]
        + [ANY] * 8,
        scratch_shapes=piece_scratch(x[0]),
        out_specs=[pl.BlockSpec((tile, width), lambda i: (i // 2, 0))] * 2
        + [pl.BlockSpec((8, width), lambda i: (0, 0))],
        out_shape=[
            jax.ShapeDtypeStruct((rows // 2, width), BF),
            jax.ShapeDtypeStruct((rows // 2, width), BF),
            jax.ShapeDtypeStruct((8, width), F32),
        ],
        compiler_params=pltpu.CompilerParams(vmem_limit_bytes=48 * 1024 * 1024),
        cost_estimate=pl.CostEstimate(
            flops=rows * width * cols // 4, bytes_accessed=rows * width, transcendentals=0
        ),
        name="pull_projections",
    )(dpre, dbeta, w, beta_w, *x)


def project_kernel(gain_ref, w_ref, beta_ref, *refs):
    n_ref, pre_ref, bpre_ref, buf, sem = refs[8:]
    x = load_piece(pl.program_id(0), refs[:8], buf, sem).astype(F32)
    unit = x * lax.rsqrt(jnp.mean(x * x, axis=-1, keepdims=True) + EPS)
    n = (unit * gain_ref[0:1, :]).astype(BF)
    n_ref[...] = n
    pre_ref[...] = mm(n, w_ref[...].reshape(-1, w_ref.shape[-1]), NN)
    bpre_ref[...] = mm(n, beta_ref[...], NN)


def project(x, gain, w, beta_w):
    tile, width = x[0].shape
    rows = 8 * tile
    groups, _, cols = w.shape

    def row(count):
        return pl.BlockSpec((tile, count), lambda i: (i, 0))

    return pl.pallas_call(
        project_kernel,
        grid=(rows // tile,),
        in_specs=[
            pl.BlockSpec((8, width), lambda i: (0, 0)),
            pl.BlockSpec((groups, width // groups, cols), lambda i: (0, 0, 0)),
            pl.BlockSpec(beta_w.shape, lambda i: (0, 0)),
        ]
        + [ANY] * 8,
        scratch_shapes=piece_scratch(x[0]),
        out_specs=[row(width), row(cols), row(beta_w.shape[1])],
        out_shape=[
            jax.ShapeDtypeStruct((rows, width), BF),
            jax.ShapeDtypeStruct((rows, cols), F32),
            jax.ShapeDtypeStruct((rows, beta_w.shape[1]), F32),
        ],
        compiler_params=pltpu.CompilerParams(vmem_limit_bytes=48 * 1024 * 1024),
        cost_estimate=pl.CostEstimate(
            flops=rows * width * cols // 4, bytes_accessed=rows * width, transcendentals=0
        ),
        name="project",
    )(gain, w, beta_w, *x)


GROUPS = 8
AXES = ("g", "a", "b", "c")
TEAM = ("a", "b", "c")
SWAP = ((0, 1), (1, 0))
CROSS = ((0, 3), (1, 2), (2, 1), (3, 0))


def swap_a(v):
    return lax.ppermute(v, "a", SWAP)


def swap_b(v):
    return lax.ppermute(v, "b", SWAP)


def swap_c(v):
    return lax.ppermute(v, "c", SWAP)


def after(v, *others):
    if not others:
        return lax.optimization_barrier(v)
    return lax.optimization_barrier((v,) + others)[0]


def plus(left, right):
    return (left.astype(F32) + right.astype(F32)).astype(BF)


def near_pieces(v):
    return v, swap_b(v), swap_a(v)


def far_piece(near):
    _, from_b, from_a = near
    rows = from_a.shape[0] // 2
    return jnp.concatenate([swap_b(from_a[:rows]), swap_a(from_b[rows:])], axis=0)


def team_pieces(near, far=None):
    pieces = []
    for v in (*near, far_piece(near) if far is None else far):
        pieces += [v, swap_c(v)]
    return pieces


def team_terms(even, odd):
    length = even.shape[0] // 4
    got = swap_c(odd)
    parts = [[v[i * length : (i + 1) * length] for v in (even, got)] for i in range(4)]
    (mine, other), *rest = parts
    return [mine.astype(F32) + other.astype(F32)] + [plus(mine, other) for mine, other in rest]


def team_start(terms, *others):
    own, near_b, near_a, far = terms
    rows = far.shape[0] // 2
    near_b, near_a, far = after((near_b, near_a, far), *others)
    via_a, via_b = swap_a(far[:rows]), swap_b(far[rows:])
    from_a, from_b = swap_a(near_a[:rows]), swap_b(near_b[rows:])
    return own, near_b[:rows], near_a[rows:], via_a, via_b, from_a, from_b


def team_end(started, *others):
    own, near_b, near_a, via_a, via_b, from_a, from_b = started
    via_a, via_b = after((via_a, via_b), *others)
    late_a = swap_a(plus(near_a, via_b))
    late_b = swap_b(plus(near_b, via_a))
    sums = jnp.concatenate(
        [
            from_a.astype(F32) + late_b.astype(F32),
            late_a.astype(F32) + from_b.astype(F32),
        ],
        axis=0,
    )
    return own + sums


def team_exchange(v):
    return lax.all_to_all(v, TEAM, 0, 0, tiled=True)


def matmul(left, right):
    return jnp.dot(left, right, preferred_element_type=F32)


def weight_grad(left, right):
    return jnp.einsum("ra,rb->ab", left, right, preferred_element_type=F32)


def back_grad(grad, weight):
    return jnp.einsum("rb,ab->ra", grad, weight, preferred_element_type=F32)


def rms_unit(value):
    scale = lax.rsqrt(jnp.mean(value * value, axis=-1, keepdims=True) + EPS)
    return value * scale, scale


def rms_pull(unit, scale, gain, grad):
    inner = grad * gain
    return scale * (inner - unit * jnp.mean(inner * unit, axis=-1, keepdims=True))


def gather_small(v, groups):
    both = v[None]
    for axis, swap in (("c", swap_c), ("b", swap_b), ("a", swap_a)):
        other = swap(both)
        mine = lax.axis_index(axis) == 0
        both = jnp.concatenate(
            [jnp.where(mine, both, other), jnp.where(mine, other, both)], axis=0
        )
    me = lax.axis_index("g")
    whole = jnp.zeros((groups,) + both.shape, both.dtype)
    whole = lax.dynamic_update_index_in_dim(whole, both, me, 0)
    for step in range(1, groups):
        got = lax.ppermute(both, "g", [(j, (j + step) % groups) for j in range(groups)])
        whole = lax.dynamic_update_index_in_dim(whole, got, (me - step) % groups, 0)
    return whole.reshape(-1, v.shape[0])


def group_sum_small(v, groups):
    me = lax.axis_index("g")
    total = lax.dynamic_index_in_dim(v, me, 0, False)
    for step in range(1, groups):
        send = lax.dynamic_index_in_dim(v, (me + step) % groups, 0, False).astype(BF)
        got = lax.ppermute(send, "g", [(j, (j + step) % groups) for j in range(groups)])
        total = total + got.astype(F32)
    return total


def group_scatter(v):
    return lax.psum_scatter(v, "g", scatter_dimension=0, tiled=True)


def group_gather(v):
    return lax.all_gather(v, "g", axis=0, tiled=False)


def on_device(
    tokens, group_ids, seq_weights, cotangent, attn_gain, w_query, w_key, w_value, w_gate, w_beta,
    conv_query, conv_key, conv_value, head_gain, w_out, mlp_gain, w_ffgate, w_ffup, w_ffdown,
):
    groups = lax.axis_size("g")
    team = 8
    devices = groups * team
    seqs, length, width = tokens.shape
    span = attn_gain.shape[0]
    taps = conv_query.shape[0]
    heads = w_beta.shape[1]
    size = head_gain.shape[0] * devices
    ff = w_ffgate.shape[1]
    cols = width // team
    own_heads = heads // team
    ff_rows = w_ffdown.shape[0]
    member = lax.axis_index(TEAM)
    first = ff_rows * groups // 2 // 128 * 128
    first = (first + 128 if first * 2 < ff_rows * groups else first) // groups
    ff_parts = [(0, first), (first, ff_rows)]

    mixer_w = jnp.concatenate(
        [w.reshape(span, team, cols) for w in (w_query, w_key, w_value, w_gate)], axis=2
    ).transpose(1, 0, 2)
    mixer_sent = team_exchange(mixer_w).reshape(team * span, 4 * cols)
    mixer_all = group_gather(
        jnp.concatenate([mixer_sent, w_out.reshape(-1, 4 * cols)], axis=0)
    )

    small = jnp.concatenate(
        [
            attn_gain, mlp_gain,
            conv_query.reshape(-1), conv_key.reshape(-1), conv_value.reshape(-1),
            head_gain, w_beta.reshape(-1),
            group_ids.astype(BF), seq_weights.astype(BF),
        ]
    )
    small = jnp.pad(small, (0, -small.shape[0] % 128))
    small = gather_small(after(small, mixer_sent), groups)

    x_own = tokens.reshape(length, width)
    x_pieces = team_pieces(near_pieces(after(x_own, mixer_sent)))
    at = 0

    def take(count):
        nonlocal at
        part = small[:, at : at + count]
        at += count
        return part

    gain_one = take(span).reshape(-1).astype(F32)
    gain_two = take(span).reshape(-1).astype(F32)
    all_taps = [
        take(taps * span).reshape(devices, taps, span).transpose(1, 0, 2).reshape(taps, width)
        for _ in range(3)
    ]
    gain_head = take(head_gain.shape[0]).reshape(-1).astype(F32)
    beta_w = take(span * heads).reshape(width, heads)
    ids = take(1).reshape(-1)
    own_taps = lax.dynamic_slice_in_dim(
        jnp.concatenate(all_taps, axis=0).astype(F32), member * cols, cols, 1
    )
    own_taps = jnp.pad(own_taps, ((0, 16 - 3 * taps), (0, 0)))
    head_rows = jnp.pad(gain_head[None], ((0, 7), (0, 0)))
    beta_w = jnp.pad(
        lax.dynamic_slice_in_dim(beta_w, member * own_heads, own_heads, 1),
        ((0, 0), (0, 128 - own_heads)),
    )
    count = jnp.sum((ids.astype(F32) == group_ids.astype(F32)[0]).astype(jnp.int32)) * length
    factor = (
        seq_weights.astype(F32)[0] * (devices * seqs * length) / (GROUPS * count.astype(F32))
    )

    ff_own = []
    gates = [w.reshape(span, groups, team, ff_rows) for w in (w_ffgate, w_ffup)]
    sent = (small, x_pieces[6])
    for low, high in ff_parts:
        part = (high - low) * groups
        main = part // 128 * 128
        own = [
            w[..., low:high].transpose(2, 0, 1, 3).reshape(team, span, part) for w in gates
        ]
        own = [w[..., :main] for w in own] + [w[..., main:] for w in own]
        own = after(jnp.concatenate(own, axis=2), *sent)
        own = team_exchange(own).reshape(team * span, 2 * part)
        sent = (own,)
        ff_own.append(own)
    d_final = cotangent.reshape(length, width).astype(F32) * factor
    d_near = near_pieces(after(d_final.astype(BF), x_pieces[6]))
    x_pieces, d_near, ff_own = after((x_pieces, d_near, ff_own))
    ff_gu = [group_gather(ff_own[0])]
    down_w = group_gather(after(w_ffdown, ff_own[0]))
    ff_gu.append(group_gather(ff_own[1]))
    ff_gu = [v.reshape(width, -1) for v in ff_gu]
    ff_down = [down_w[:, low:high].reshape(-1, width) for low, high in ff_parts]

    gain_rows = jnp.pad(gain_one[None], ((0, 7), (0, 0)))
    normed, pre, beta_pre = project(x_pieces, gain_rows, mixer_all, beta_w)
    place = member.astype(jnp.int32).reshape(1)
    out_near = near_pieces(mixer_all[:, team * span :].reshape(groups * span, width))
    pre, out_near = after((pre, out_near))
    gated, inverse = delta_forward(
        place, pre, beta_pre, own_taps, head_rows, team, own_heads, size
    )
    d_down = team_pieces(after(d_near, out_near))
    gated, d_down[6], out_near = after((gated, d_down[6], out_near))
    gated, out_far = after((team_exchange(gated), far_piece(out_near)))
    out_pieces = [v.reshape(groups, span, width) for v in team_pieces(out_near, out_far)]
    gated = gated.transpose(1, 0, 2).reshape(length, width)
    out_full = assemble(place, out_pieces).reshape(width, width)
    inputs = x_own.astype(F32)
    resid = inputs + matmul(gated, out_full)

    unit_two, scale_two = rms_unit(resid)
    normed_two = team_pieces(near_pieces((unit_two * gain_two).astype(BF)))
    normed_two, d_down, hidden, d_gu, *sums = feed_forward(
        ff_gu[0], ff_down[0], normed_two, d_down
    )
    grad_gu = weight_grad(normed_two, d_gu).astype(BF)
    hidden_more, d_gu_more, dn_even, dn_odd, out_even, out_odd = feed_forward(
        ff_gu[1], ff_down[1], more=(normed_two, d_down) + tuple(after(sums, grad_gu))
    )
    ff_grads = [group_scatter(grad_gu)]
    terms = team_terms(dn_even, dn_odd)
    hidden, hidden_more = after((hidden, hidden_more), *terms)
    grad_gu = weight_grad(normed_two, d_gu_more).astype(BF)
    ff_grads.append(group_scatter(grad_gu))
    grad_down = jnp.concatenate(
        [
            weight_grad(v, d_down).astype(BF).reshape(groups, -1, width)
            for v in after((hidden, hidden_more), grad_gu)
        ],
        axis=1,
    )
    final_terms = team_terms(*after((out_even, out_odd), *terms))
    started = team_start(terms)
    started, grad_down, ff_grads[0] = after((started, grad_down, ff_grads[0]))
    grad_ffdown = group_scatter(grad_down.reshape(-1, width)).astype(F32)
    d_normed_two = team_end(started)
    gu_home_first = team_exchange(after(ff_grads[0], d_normed_two))
    mlp_part = jnp.sum(d_normed_two * unit_two, axis=0)
    d_resid = d_final + rms_pull(unit_two, scale_two, gain_two, d_normed_two)

    d_branch = d_resid.astype(BF)
    d_gated = back_grad(d_branch, out_full).astype(BF)
    d_gated_sent = d_gated.reshape(length, team, cols).transpose(1, 0, 2)
    d_gated_sent, gu_home_first = after((d_gated_sent, gu_home_first))
    d_gated = team_exchange(d_gated_sent)
    final_started = team_start(final_terms, d_gated)
    gated_rows = gated.reshape(length, groups, team, span)
    gated_rows = [
        lax.dynamic_index_in_dim(gated_rows, jnp.bitwise_xor(member, i), 2, False).reshape(
            length, groups * span
        )
        for i in range(team)
    ]
    out_terms = team_terms(
        *[
            weight_grad(jnp.concatenate(gated_rows[i::2], axis=1), d_branch).astype(BF)
            for i in range(2)
        ]
    )
    d_pre, d_beta, d_taps, d_head = delta_backward(
        place, pre, beta_pre, own_taps, head_rows, inverse, after(d_gated, *out_terms), team,
        own_heads, size
    )
    d_pre, final_started = after((d_pre, final_started))
    final_sum = team_end(final_started)
    grads = weight_grad(normed, d_pre).astype(BF)
    mixer_grads = group_scatter(grads)
    d_pre, grads, final_sum, ff_grads[1] = after((d_pre, grads, final_sum, ff_grads[1]))
    out_started = team_start(out_terms, final_sum)
    grad_beta = weight_grad(normed, d_beta)[:, :own_heads]
    dn_even, dn_odd, attn_part = pull_projections(
        d_pre, d_beta, x_pieces, mixer_all, beta_w
    )
    dn_even, dn_odd, out_started, grad_ffdown = after((dn_even, dn_odd, out_started, grad_ffdown))
    grad_out = team_end(out_started)
    in_terms = team_terms(dn_even, dn_odd)
    grad_out_home = group_sum_small(grad_out.reshape(groups, span, width), groups)
    mixed = (resid + final_sum).astype(BF).reshape(seqs, length, width)
    in_terms, mixer_grads = after((in_terms, mixer_grads))
    in_started = team_start(in_terms, out_started)
    gu_home = [gu_home_first, team_exchange(after(ff_grads[1], *in_terms[1:]))]

    ff_home = [[], []]
    for gu, (low, high) in zip(gu_home, ff_parts):
        part = (high - low) * groups
        main = part // 128 * 128
        gu = after(gu, mixer_grads).reshape(team, span, 2 * part)
        gate = jnp.concatenate([gu[..., :main], gu[..., 2 * main : part + main]], axis=2)
        up = jnp.concatenate([gu[..., main : 2 * main], gu[..., part + main :]], axis=2)
        for home, v in zip(ff_home, (gate, up)):
            home.append(v.reshape(team, span, groups, high - low).transpose(1, 2, 0, 3))
    grad_ffgate, grad_ffup = [
        jnp.concatenate(home, axis=3).reshape(span, ff).astype(F32) for home in ff_home
    ]
    mixer_grads = team_exchange(mixer_grads)
    mixer_grads = mixer_grads.reshape(team, span, 4, cols).transpose(2, 1, 0, 3)
    mixer_grads = mixer_grads.reshape(4, span, width).astype(F32)

    tap_rows = lax.dynamic_update_slice_in_dim(
        jnp.zeros((3 * taps, width), F32), d_taps[: 3 * taps], member * cols, 1
    )
    head_part = jnp.pad(
        d_head[0].reshape(devices, -1), ((0, 0), (0, span - head_gain.shape[0]))
    )
    extra = jnp.concatenate(
        [
            grad_beta, jnp.sum(attn_part, axis=0)[:, None], tap_rows.T,
            head_part.reshape(-1)[:, None], mlp_part[:, None],
        ],
        axis=1,
    )
    kinds = extra.shape[1]
    extra = extra.reshape(groups, team, span * kinds)
    extra = jnp.pad(extra, ((0, 0), (0, 0), (0, -extra.shape[2] % 128)))
    extra = team_exchange(group_sum_small(extra, groups))
    extra = extra[:, : span * kinds].reshape(team, span, kinds)
    grad_beta = extra[:, :, :own_heads].transpose(1, 0, 2).reshape(span, heads)
    rest = jnp.sum(extra[:, :, own_heads:], axis=0)
    grad_attn = rest[:, 0]
    grad_taps = rest[:, 1 : 1 + 3 * taps].T.reshape(3, taps, span)
    grad_head = rest[: head_gain.shape[0], 1 + 3 * taps]
    grad_mlp = rest[:, 2 + 3 * taps]

    d_normed = team_end(in_started)
    unit_one, scale_one = rms_unit(inputs)
    input_grad = d_resid + rms_pull(unit_one, scale_one, gain_one, d_normed)
    return (
        mixed,
        input_grad.reshape(seqs, length, width),
        grad_attn,
        mixer_grads[0],
        mixer_grads[1],
        mixer_grads[2],
        mixer_grads[3],
        grad_beta,
        grad_taps[0],
        grad_taps[1],
        grad_taps[2],
        grad_head,
        grad_out_home,
        grad_mlp,
        grad_ffgate,
        grad_ffup,
        grad_ffdown,
    )


def solution(mesh):
    dp, fsdp = mesh.shape["dp"], mesh.shape["fsdp"]
    finer = jax.sharding.Mesh(mesh.devices.reshape(dp // 2, 2, fsdp // 2, 2), AXES)
    one, rows, last = P(AXES), P(AXES, None), P(None, AXES)
    seq = P(AXES, None, None)
    return jax.shard_map(
        on_device,
        mesh=finer,
        in_specs=(
            seq, one, one, seq, one, rows, rows, rows, rows, rows, last, last, last, one, rows,
            one, rows, rows, rows,
        ),
        out_specs=(
            seq, seq, one, rows, rows, rows, rows, rows, last, last, last, one, rows, one, rows,
            rows, rows,
        ),
        check_vma=False,
    )
```

```python
import collections
import functools
import jax
import jax.numpy as jnp
from jax import lax
from jax.experimental import pallas as pl
from jax.experimental.pallas import tpu as pltpu
from jax.sharding import PartitionSpec as P

EPS = 1e-06
BF = jnp.bfloat16
F32 = jnp.float32


def mm(left, right, dims):
    return lax.dot_general(left, right, ((dims[0], dims[1]), ((), ())), preferred_element_type=F32)


NN = ((1,), (0,))
NT = ((1,), (1,))
TN = ((0,), (0,))


def halves(value):
    high = value.astype(BF)
    return high, (value - high.astype(F32)).astype(BF)


def mm3(left, right, dims):
    lh, ll = left
    rh, rl = right
    return mm(lh, rh, dims) + (mm(lh, rl, dims) + mm(ll, rh, dims))


def mm2(left, right, dims):
    lh, ll = left
    return mm(lh, right, dims) + mm(ll, right, dims)


def sigmoid(v):
    return 1.0 / (1.0 + jnp.exp(-v))


def shift_down(v, count, rows):
    if count == 0:
        return v
    return jnp.where(rows >= count, pltpu.roll(v, count, 0), 0.0)


def shift_up(v, count, rows):
    if count == 0:
        return v
    length = v.shape[0]
    return jnp.where(rows < length - count, pltpu.roll(v, length - count, 0), 0.0)


def conv_of(pre, taps, rows):
    total = taps[0] * pre
    for j in range(1, len(taps)):
        total = total + taps[j] * shift_down(pre, j, rows)
    return total


def unit_inverses(stricts):
    size = stricts[0].shape[0]
    ri = lax.broadcasted_iota(jnp.int32, (size, size), 0)
    ci = lax.broadcasted_iota(jnp.int32, (size, size), 1)
    diff = jnp.bitwise_xor(ri, ci)
    eye = jnp.where(ri == ci, 1.0, 0.0)
    results = [eye - jnp.where(diff == 1, strict, 0.0) for strict in stricts]
    span = 2
    while span < size:
        here = (diff >= span) & (diff < 2 * span)
        split = [halves(result) for result in results]
        inner = [mm3(halves(jnp.where(here, s, 0.0)), r, NN) for s, r in zip(stricts, split)]
        inner = [halves(i) for i in inner]
        results = [t - mm3(r, i, NN) for t, r, i in zip(results, split, inner)]
        span *= 2
    return results


def head_forward(pre_q, pre_k, pre_v, beta_pre, taps):
    length, size = pre_q.shape
    rows = lax.broadcasted_iota(jnp.int32, (length, size), 0)
    cq = conv_of(pre_q, taps[0:4], rows)
    ck = conv_of(pre_k, taps[4:8], rows)
    cv = conv_of(pre_v, taps[8:12], rows)
    sq, sk, sv = sigmoid(cq), sigmoid(ck), sigmoid(cv)
    yq, yk, yv = cq * sq, ck * sk, cv * sv
    rq = lax.rsqrt(jnp.sum(yq * yq, axis=-1, keepdims=True) + EPS)
    rk = lax.rsqrt(jnp.sum(yk * yk, axis=-1, keepdims=True) + EPS)
    query = (yq * rq * size ** (-0.5)).astype(BF)
    key = (yk * rk).astype(BF)
    value = yv.astype(BF)
    beta = sigmoid(beta_pre)
    return (cq, ck, cv, sq, sk, sv, yq, yk, rq, rk, query, key, value, beta, rows)


def lower_masks(length):
    ri = lax.broadcasted_iota(jnp.int32, (length, length), 0)
    ci = lax.broadcasted_iota(jnp.int32, (length, length), 1)
    return ri > ci, ri >= ci


def fwd_kernel(
    place_ref, pre_ref, bpre_ref, taps_ref, gain_ref, gated_ref, inv_ref, *, heads, size, length
):
    half = length // 2
    width = heads * size
    flip = place_ref[0] & (gated_ref.shape[0] - 1)
    strictly, inclusive = lower_masks(length)
    work = []
    blocks = []
    chains = [(b, h) for b in range(pre_ref.shape[0] // length) for h in range(heads)]
    for b, h in chains:
        at = pl.ds(h * size, size)
        rows = pl.ds(b * length, length)
        pre = [pre_ref[rows, pl.ds(i * width + h * size, size)] for i in range(3)]
        taps = [taps_ref[i : i + 1, at] for i in range(12)]
        made = head_forward(*pre, bpre_ref[rows, h : h + 1], taps)
        query, key, value, beta = made[10:14]
        strict = jnp.where(strictly, mm(key, key, NT) * beta, 0.0)
        blocks += [strict[:half, :half], strict[half:, half:]]
        scores = jnp.where(inclusive, mm(query, key, NT), 0.0)
        work.append((halves(strict[half:, :half]), value.astype(F32) * beta, halves(scores)))
    inverses = unit_inverses(blocks)
    for n, (b, h) in enumerate(chains):
        inv_ref[b, h, 0] = inverses[2 * n]
        inv_ref[b, h, 1] = inverses[2 * n + 1]
    tops = [mm3(halves(inverses[2 * n]), halves(w[1][:half]), NN) for n, w in enumerate(work)]
    lows = [w[1][half:] - mm3(w[0], halves(top), NN) for w, top in zip(work, tops)]
    lows = [mm3(halves(inverses[2 * n + 1]), halves(low), NN) for n, low in enumerate(lows)]
    mixers = [
        mm3(w[2], halves(jnp.concatenate([top, low], axis=0)), NN)
        for w, top, low in zip(work, tops, lows)
    ]
    for (b, h), mixer in zip(chains, mixers):
        at = pl.ds(h * size, size)
        rows = pl.ds(b * length, length)
        scale = lax.rsqrt(jnp.mean(mixer * mixer, axis=-1, keepdims=True) + EPS)
        gate = pre_ref[rows, pl.ds(3 * width + h * size, size)]
        gated = mixer * scale * gain_ref[0:1, :] * (gate * sigmoid(gate))
        gated_ref[b ^ flip, :, at] = gated.astype(BF)


def bwd_chain(refs, b, h, heads, size, length, masks, sums):
    pre_ref, bpre_ref, taps_ref, gain_ref, inv_ref, dgated_ref, dpre_ref, dbeta_ref, flip = refs
    strictly, inclusive = masks
    half = length // 2
    width = heads * size
    at = pl.ds(h * size, size)
    line = pl.ds(b * length, length)
    cols = [pl.ds(i * width + h * size, size) for i in range(4)]
    taps = [taps_ref[i : i + 1, at] for i in range(12)]
    made = head_forward(
        *[pre_ref[line, c] for c in cols[:3]], bpre_ref[line, h : h + 1], taps
    )
    (cq, ck, cv, sq, sk, sv, yq, yk, rq, rk, query, key, value, beta, rows) = made
    yield
    gram = mm(key, key, NT)
    cross = halves((gram * beta)[half:, :half])
    scores = halves(jnp.where(inclusive, mm(query, key, NT), 0.0))
    top, low = halves(inv_ref[b, h, 0]), halves(inv_ref[b, h, 1])
    val = value.astype(F32)
    rhs = val * beta
    yield
    fresh_top = mm3(top, halves(rhs[:half]), NN)
    yield
    fresh_low = rhs[half:] - mm3(cross, halves(fresh_top), NN)
    yield
    fresh_low = mm3(low, halves(fresh_low), NN)
    fresh = halves(jnp.concatenate([fresh_top, fresh_low], axis=0))
    yield
    mixer = mm3(scores, fresh, NN)
    yield
    scale = lax.rsqrt(jnp.mean(mixer * mixer, axis=-1, keepdims=True) + EPS)
    gate = pre_ref[line, cols[3]]
    sg = sigmoid(gate)
    dgated = dgated_ref[b ^ flip, :, at].astype(F32)
    unit = mixer * scale
    gain = gain_ref[0:1, :]
    dgate = dgated * unit * gain * (sg * (1.0 + gate * (1.0 - sg)))
    dnorm = dgated * (gate * sg)
    sums["gain"].append(jnp.sum(dnorm * unit, axis=0, keepdims=True))
    dunit = dnorm * gain
    dmixer = scale * (dunit - unit * jnp.mean(dunit * unit, axis=-1, keepdims=True))
    dm = halves(dmixer)
    dpre_ref[line, cols[3]] = dgate.astype(BF)
    yield
    dscores = halves(jnp.where(inclusive, mm3(dm, fresh, NT), 0.0))
    dfresh = mm3(scores, dm, TN)
    yield
    drhs_low = mm3(low, halves(dfresh[half:]), TN)
    yield
    drhs_top = dfresh[:half] - mm3(cross, halves(drhs_low), TN)
    yield
    drhs_top = mm3(top, halves(drhs_top), TN)
    drhs = jnp.concatenate([drhs_top, drhs_low], axis=0)
    yield
    dstrict = jnp.where(strictly, -mm3(halves(drhs), fresh, NT), 0.0)
    dgram = halves(dstrict * beta)
    dval = drhs * beta
    dbeta = jnp.sum(dstrict * gram, axis=-1, keepdims=True) + jnp.sum(
        drhs * val, axis=-1, keepdims=True
    )
    dbeta_ref[line, h : h + 1] = (dbeta * beta * (1.0 - beta)).astype(BF)
    yield
    dquery = mm2(dscores, key, NN)
    dkey = mm2(dscores, query, TN) + mm2(dgram, key, NN) + mm2(dgram, key, TN)
    yield
    sc = size ** (-0.5)
    uq, uk = yq * rq, yk * rk
    dyq = (rq * sc) * (dquery - uq * jnp.sum(dquery * uq, axis=-1, keepdims=True))
    dyk = rk * (dkey - uk * jnp.sum(dkey * uk, axis=-1, keepdims=True))
    for i, (dy, s, c) in enumerate(((dyq, sq, cq), (dyk, sk, ck), (dval, sv, cv))):
        dc = dy * (s * (1.0 + c * (1.0 - s)))
        total = taps[4 * i] * dc
        for j in range(4):
            moved = shift_down(pre_ref[line, cols[i]], j, rows)
            sums[4 * i + j, h].append(jnp.sum(dc * moved, axis=0, keepdims=True))
            if j:
                total = total + taps[4 * i + j] * shift_up(dc, j, rows)
        dpre_ref[line, cols[i]] = total.astype(BF)
        yield


def bwd_kernel(
    place_ref, pre_ref, bpre_ref, taps_ref, gain_ref, inv_ref, dgated_ref,
    dpre_ref, dbeta_ref, dtaps_ref, dgain_ref, *, heads, size, length,
):
    @pl.when(pl.program_id(0) == 0)
    def _():
        dtaps_ref[...] = jnp.zeros_like(dtaps_ref)
        dgain_ref[...] = jnp.zeros_like(dgain_ref)

    dbeta_ref[...] = jnp.zeros_like(dbeta_ref)
    masks = lower_masks(length)
    sums = collections.defaultdict(list)
    flip = place_ref[0] & (dgated_ref.shape[0] - 1)
    refs = (
        pre_ref, bpre_ref, taps_ref, gain_ref, inv_ref, dgated_ref, dpre_ref, dbeta_ref, flip
    )
    chains = [
        bwd_chain(refs, b, h, heads, size, length, masks, sums)
        for b in range(dgated_ref.shape[0])
        for h in range(heads)
    ]
    while chains:
        chains = [chain for chain in chains if next(chain, True) is None]
    dgain_ref[0:1, :] += sum(sums.pop("gain"))
    for (row, h), parts in sums.items():
        dtaps_ref[row : row + 1, pl.ds(h * size, size)] += sum(parts)


PAIR = 2


def team_block(i, p):
    return (jnp.bitwise_xor(p[0] // PAIR, i), 0, 0)


def delta_forward(place, pre, bpre, taps, gain, slots, heads, size):
    rows = pre.shape[0]
    length = rows // slots
    width = heads * size
    return pl.pallas_call(
        functools.partial(fwd_kernel, heads=heads, size=size, length=length),
        grid_spec=pltpu.PrefetchScalarGridSpec(
            num_scalar_prefetch=1,
            grid=(slots // PAIR,),
            in_specs=[
                pl.BlockSpec((PAIR * length, 4 * width), lambda i, p: (i, 0)),
                pl.BlockSpec((PAIR * length, 128), lambda i, p: (i, 0)),
                pl.BlockSpec((16, width), lambda i, p: (0, 0)),
                pl.BlockSpec((8, size), lambda i, p: (0, 0)),
            ],
            out_specs=[
                pl.BlockSpec((PAIR, length, width), team_block),
                pl.BlockSpec((PAIR, heads, 2, length // 2, length // 2), lambda i, p: (i, 0, 0, 0, 0)),
            ],
        ),
        out_shape=[
            jax.ShapeDtypeStruct((slots, length, width), BF),
            jax.ShapeDtypeStruct((slots, heads, 2, length // 2, length // 2), F32),
        ],
        compiler_params=pltpu.CompilerParams(vmem_limit_bytes=48 * 1024 * 1024),
        cost_estimate=pl.CostEstimate(
            flops=slots * heads * 100_000_000, bytes_accessed=rows * width * 4, transcendentals=0
        ),
        name="delta_forward",
    )(place, pre, bpre, taps, gain)


def delta_backward(place, pre, bpre, taps, gain, inverse, dgated, slots, heads, size):
    rows = pre.shape[0]
    length = rows // slots
    width = heads * size
    return pl.pallas_call(
        functools.partial(bwd_kernel, heads=heads, size=size, length=length),
        grid_spec=pltpu.PrefetchScalarGridSpec(
            num_scalar_prefetch=1,
            grid=(slots // PAIR,),
            in_specs=[
                pl.BlockSpec((PAIR * length, 4 * width), lambda i, p: (i, 0)),
                pl.BlockSpec((PAIR * length, 128), lambda i, p: (i, 0)),
                pl.BlockSpec((16, width), lambda i, p: (0, 0)),
                pl.BlockSpec((8, size), lambda i, p: (0, 0)),
                pl.BlockSpec((PAIR, heads, 2, length // 2, length // 2), lambda i, p: (i, 0, 0, 0, 0)),
                pl.BlockSpec((PAIR, length, width), team_block),
            ],
            out_specs=[
                pl.BlockSpec((PAIR * length, 4 * width), lambda i, p: (i, 0)),
                pl.BlockSpec((PAIR * length, 128), lambda i, p: (i, 0)),
                pl.BlockSpec((16, width), lambda i, p: (0, 0)),
                pl.BlockSpec((8, size), lambda i, p: (0, 0)),
            ],
        ),
        out_shape=[
            jax.ShapeDtypeStruct((rows, 4 * width), BF),
            jax.ShapeDtypeStruct((rows, 128), BF),
            jax.ShapeDtypeStruct((16, width), F32),
            jax.ShapeDtypeStruct((8, size), F32),
        ],
        compiler_params=pltpu.CompilerParams(vmem_limit_bytes=48 * 1024 * 1024),
        cost_estimate=pl.CostEstimate(
            flops=slots * heads * 100_000_000, bytes_accessed=rows * width * 4, transcendentals=0
        ),
        name="delta_backward",
    )(place, pre, bpre, taps, gain, inverse, dgated)


def load_piece(step, pieces, buf, sem):
    def start(which):
        for n, piece in enumerate(pieces):

            @pl.when(which == n)
            def _():
                pltpu.make_async_copy(piece, buf.at[n % 2], sem.at[n % 2]).start()

    @pl.when(step == 0)
    def _():
        start(0)

    start(step + 1)
    slot = lax.rem(step, 2)
    pltpu.make_async_copy(pieces[0], buf.at[slot], sem.at[slot]).wait()
    return buf[slot]


def piece_scratch(piece):
    return [pltpu.VMEM((2,) + piece.shape, piece.dtype), pltpu.SemaphoreType.DMA((2,))]


ANY = pl.BlockSpec(memory_space=pl.ANY)


def assemble_kernel(place_ref, *refs):
    *pieces, out_ref, buf, sem = refs
    out_ref[:, 0] = load_piece(pl.program_id(0), pieces, buf, sem)


def assemble(place, pieces):
    groups, rows, width = pieces[0].shape
    count = len(pieces)
    return pl.pallas_call(
        assemble_kernel,
        grid_spec=pltpu.PrefetchScalarGridSpec(
            num_scalar_prefetch=1,
            grid=(count,),
            in_specs=[ANY] * count,
            out_specs=pl.BlockSpec(
                (groups, 1, rows, width), lambda i, p: (0, jnp.bitwise_xor(p[0], i), 0, 0)
            ),
            scratch_shapes=piece_scratch(pieces[0]),
        ),
        out_shape=jax.ShapeDtypeStruct((groups, count, rows, width), BF),
        cost_estimate=pl.CostEstimate(
            flops=0, bytes_accessed=4 * count * groups * rows * width, transcendentals=0
        ),
        name="assemble",
    )(place, *pieces)


def ff_tile(n, d, gu_ref, down_ref, hid_ref, dgu_ref):
    cols = hid_ref.shape[1]
    main = cols // 128 * 128
    gu_w = gu_ref[...]
    gu = mm(n, gu_w, NN)
    dh = mm(d, down_ref[...], NT)
    spans = [(0, main, main, 0)]
    if main < cols:
        spans.append((2 * main, main + cols, cols - main, main))
    for gate_at, up_at, count, at in spans:
        gate, up = gu[:, gate_at : gate_at + count], gu[:, up_at : up_at + count]
        grad = dh[:, at : at + count]
        sig = sigmoid(gate)
        silu = gate * sig
        hid_ref[:, at : at + count] = (silu * up).astype(BF)
        dgu_ref[:, gate_at : gate_at + count] = (grad * up * (sig + silu * (1.0 - sig))).astype(BF)
        dgu_ref[:, up_at : up_at + count] = (grad * silu).astype(BF)
    return mm(dgu_ref[...], gu_w, NT), mm(hid_ref[...], down_ref[...], NN)


def ff_first_kernel(gu_ref, down_ref, *refs):
    ns, ds = refs[:8], refs[8:16]
    n_ref, d_ref, hid_ref, dgu_ref, dn_ref, out_ref, n_buf, n_sem, d_buf, d_sem = refs[16:]
    step = pl.program_id(0)
    n = load_piece(step, ns, n_buf, n_sem)
    d = load_piece(step, ds, d_buf, d_sem)
    n_ref[...] = n
    d_ref[...] = d
    dn, out = ff_tile(n, d, gu_ref, down_ref, hid_ref, dgu_ref)
    dn_ref[...] = dn.astype(BF)
    out_ref[...] = out.astype(BF)


def put_pair(step, value, even_ref, odd_ref):
    value = value.astype(BF)

    @pl.when(lax.rem(step, 2) == 0)
    def _():
        even_ref[...] = value

    @pl.when(lax.rem(step, 2) == 1)
    def _():
        odd_ref[...] = value


def ff_more_kernel(
    gu_ref, down_ref, n_ref, d_ref, dn_in, out_in,
    hid_ref, dgu_ref, dn_even, dn_odd, out_even, out_odd,
):
    dn, out = ff_tile(n_ref[...], d_ref[...], gu_ref, down_ref, hid_ref, dgu_ref)
    step = pl.program_id(0)
    put_pair(step, dn + dn_in[...].astype(F32), dn_even, dn_odd)
    put_pair(step, out + out_in[...].astype(F32), out_even, out_odd)


def feed_forward(gu, down, ns=None, ds=None, more=None):
    cols, width = down.shape
    tile = ns[0].shape[0] if more is None else more[0].shape[0] // 8
    rows = 8 * tile

    def row(count):
        return pl.BlockSpec((tile, count), lambda i: (i, 0))

    pair = pl.BlockSpec((tile, width), lambda i: (i // 2, 0))
    if more is None:
        outs = [width, width, cols, 2 * cols, width, width]
        out_specs = [row(k) for k in outs]
        shapes = [(rows, k) for k in outs]
    else:
        out_specs = [row(cols), row(2 * cols)] + [pair] * 4
        shapes = [(rows, cols), (rows, 2 * cols)] + [(rows // 2, width)] * 4
    return pl.pallas_call(
        ff_first_kernel if more is None else ff_more_kernel,
        grid=(8,),
        in_specs=[
            pl.BlockSpec((width, 2 * cols), lambda i: (0, 0)),
            pl.BlockSpec((cols, width), lambda i: (0, 0)),
        ]
        + ([ANY] * 16 if more is None else [row(width)] * 4),
        out_specs=out_specs,
        out_shape=[jax.ShapeDtypeStruct(k, BF) for k in shapes],
        scratch_shapes=piece_scratch(ns[0]) + piece_scratch(ds[0]) if more is None else [],
        compiler_params=pltpu.CompilerParams(vmem_limit_bytes=56 * 1024 * 1024),
        cost_estimate=pl.CostEstimate(
            flops=rows * width * cols, bytes_accessed=2 * rows * width, transcendentals=0
        ),
        name="feed_forward",
    )(gu, down, *(tuple(ns) + tuple(ds) if more is None else more))


def pull_kernel(dpre_ref, dbeta_ref, w_ref, beta_ref, *refs):
    even_ref, odd_ref, part_ref, buf, sem = refs[8:]

    @pl.when(pl.program_id(0) == 0)
    def _():
        part_ref[...] = jnp.zeros_like(part_ref)

    x = load_piece(pl.program_id(0), refs[:8], buf, sem).astype(F32)
    unit = x * lax.rsqrt(jnp.mean(x * x, axis=-1, keepdims=True) + EPS)
    w = w_ref[...].reshape(-1, w_ref.shape[-1])
    dn = mm(dpre_ref[...], w, NT) + mm(dbeta_ref[...], beta_ref[...], NT)
    part_ref[...] += jnp.sum((dn * unit).reshape(-1, 8, dn.shape[1]), axis=0)
    put_pair(pl.program_id(0), dn, even_ref, odd_ref)


def pull_projections(dpre, dbeta, x, w, beta_w):
    tile, width = x[0].shape
    rows, cols = dpre.shape
    groups = w.shape[0]

    def row(count):
        return pl.BlockSpec((tile, count), lambda i: (i, 0))

    return pl.pallas_call(
        pull_kernel,
        grid=(rows // tile,),
        in_specs=[
            row(cols),
            row(dbeta.shape[1]),
            pl.BlockSpec((groups, width // groups, cols), lambda i: (0, 0, 0)),
            pl.BlockSpec(beta_w.shape, lambda i: (0, 0)),
        ]
        + [ANY] * 8,
        scratch_shapes=piece_scratch(x[0]),
        out_specs=[pl.BlockSpec((tile, width), lambda i: (i // 2, 0))] * 2
        + [pl.BlockSpec((8, width), lambda i: (0, 0))],
        out_shape=[
            jax.ShapeDtypeStruct((rows // 2, width), BF),
            jax.ShapeDtypeStruct((rows // 2, width), BF),
            jax.ShapeDtypeStruct((8, width), F32),
        ],
        compiler_params=pltpu.CompilerParams(vmem_limit_bytes=48 * 1024 * 1024),
        cost_estimate=pl.CostEstimate(
            flops=rows * width * cols // 4, bytes_accessed=rows * width, transcendentals=0
        ),
        name="pull_projections",
    )(dpre, dbeta, w, beta_w, *x)


def project_kernel(gain_ref, w_ref, beta_ref, *refs):
    n_ref, pre_ref, bpre_ref, buf, sem = refs[8:]
    x = load_piece(pl.program_id(0), refs[:8], buf, sem).astype(F32)
    unit = x * lax.rsqrt(jnp.mean(x * x, axis=-1, keepdims=True) + EPS)
    n = (unit * gain_ref[0:1, :]).astype(BF)
    n_ref[...] = n
    pre_ref[...] = mm(n, w_ref[...].reshape(-1, w_ref.shape[-1]), NN)
    bpre_ref[...] = mm(n, beta_ref[...], NN)


def project(x, gain, w, beta_w):
    tile, width = x[0].shape
    rows = 8 * tile
    groups, _, cols = w.shape

    def row(count):
        return pl.BlockSpec((tile, count), lambda i: (i, 0))

    return pl.pallas_call(
        project_kernel,
        grid=(rows // tile,),
        in_specs=[
            pl.BlockSpec((8, width), lambda i: (0, 0)),
            pl.BlockSpec((groups, width // groups, cols), lambda i: (0, 0, 0)),
            pl.BlockSpec(beta_w.shape, lambda i: (0, 0)),
        ]
        + [ANY] * 8,
        scratch_shapes=piece_scratch(x[0]),
        out_specs=[row(width), row(cols), row(beta_w.shape[1])],
        out_shape=[
            jax.ShapeDtypeStruct((rows, width), BF),
            jax.ShapeDtypeStruct((rows, cols), F32),
            jax.ShapeDtypeStruct((rows, beta_w.shape[1]), F32),
        ],
        compiler_params=pltpu.CompilerParams(vmem_limit_bytes=48 * 1024 * 1024),
        cost_estimate=pl.CostEstimate(
            flops=rows * width * cols // 4, bytes_accessed=rows * width, transcendentals=0
        ),
        name="project",
    )(gain, w, beta_w, *x)


GROUPS = 8
AXES = ("g", "a", "b", "c")
TEAM = ("a", "b", "c")
SWAP = ((0, 1), (1, 0))
CROSS = ((0, 3), (1, 2), (2, 1), (3, 0))


def swap_a(v):
    return lax.ppermute(v, "a", SWAP)


def swap_b(v):
    return lax.ppermute(v, "b", SWAP)


def swap_c(v):
    return lax.ppermute(v, "c", SWAP)


def after(v, *others):
    if not others:
        return lax.optimization_barrier(v)
    return lax.optimization_barrier((v,) + others)[0]


def plus(left, right):
    return (left.astype(F32) + right.astype(F32)).astype(BF)


def near_pieces(v):
    return v, swap_b(v), swap_a(v)


def far_piece(near):
    _, from_b, from_a = near
    rows = from_a.shape[0] // 2
    return jnp.concatenate([swap_b(from_a[:rows]), swap_a(from_b[rows:])], axis=0)


def team_pieces(near, far=None):
    pieces = []
    for v in (*near, far_piece(near) if far is None else far):
        pieces += [v, swap_c(v)]
    return pieces


def team_terms(even, odd):
    length = even.shape[0] // 4
    got = swap_c(odd)
    parts = [[v[i * length : (i + 1) * length] for v in (even, got)] for i in range(4)]
    (mine, other), *rest = parts
    return [mine.astype(F32) + other.astype(F32)] + [plus(mine, other) for mine, other in rest]


def team_start(terms, *others):
    own, near_b, near_a, far = terms
    rows = far.shape[0] // 2
    near_b, near_a, far = after((near_b, near_a, far), *others)
    via_a, via_b = swap_a(far[:rows]), swap_b(far[rows:])
    from_a, from_b = swap_a(near_a[:rows]), swap_b(near_b[rows:])
    return own, near_b[:rows], near_a[rows:], via_a, via_b, from_a, from_b


def team_end(started, *others):
    own, near_b, near_a, via_a, via_b, from_a, from_b = started
    via_a, via_b = after((via_a, via_b), *others)
    late_a = swap_a(plus(near_a, via_b))
    late_b = swap_b(plus(near_b, via_a))
    sums = jnp.concatenate(
        [
            from_a.astype(F32) + late_b.astype(F32),
            late_a.astype(F32) + from_b.astype(F32),
        ],
        axis=0,
    )
    return own + sums


def team_exchange(v):
    return lax.all_to_all(v, TEAM, 0, 0, tiled=True)


def matmul(left, right):
    return jnp.dot(left, right, preferred_element_type=F32)


def weight_grad(left, right):
    return jnp.einsum("ra,rb->ab", left, right, preferred_element_type=F32)


def back_grad(grad, weight):
    return jnp.einsum("rb,ab->ra", grad, weight, preferred_element_type=F32)


def rms_unit(value):
    scale = lax.rsqrt(jnp.mean(value * value, axis=-1, keepdims=True) + EPS)
    return value * scale, scale


def rms_pull(unit, scale, gain, grad):
    inner = grad * gain
    return scale * (inner - unit * jnp.mean(inner * unit, axis=-1, keepdims=True))


def gather_small(v, groups):
    both = v[None]
    for axis, swap in (("c", swap_c), ("b", swap_b), ("a", swap_a)):
        other = swap(both)
        mine = lax.axis_index(axis) == 0
        both = jnp.concatenate(
            [jnp.where(mine, both, other), jnp.where(mine, other, both)], axis=0
        )
    me = lax.axis_index("g")
    whole = jnp.zeros((groups,) + both.shape, both.dtype)
    whole = lax.dynamic_update_index_in_dim(whole, both, me, 0)
    for step in range(1, groups):
        got = lax.ppermute(both, "g", [(j, (j + step) % groups) for j in range(groups)])
        whole = lax.dynamic_update_index_in_dim(whole, got, (me - step) % groups, 0)
    return whole.reshape(-1, v.shape[0])


def group_sum_small(v, groups):
    me = lax.axis_index("g")
    total = lax.dynamic_index_in_dim(v, me, 0, False)
    for step in range(1, groups):
        send = lax.dynamic_index_in_dim(v, (me + step) % groups, 0, False).astype(BF)
        got = lax.ppermute(send, "g", [(j, (j + step) % groups) for j in range(groups)])
        total = total + got.astype(F32)
    return total


def group_scatter(v):
    return lax.psum_scatter(v, "g", scatter_dimension=0, tiled=True)


def group_gather(v):
    return lax.all_gather(v, "g", axis=0, tiled=False)


def on_device(
    tokens, group_ids, seq_weights, cotangent, attn_gain, w_query, w_key, w_value, w_gate, w_beta,
    conv_query, conv_key, conv_value, head_gain, w_out, mlp_gain, w_ffgate, w_ffup, w_ffdown,
):
    groups = lax.axis_size("g")
    team = 8
    devices = groups * team
    seqs, length, width = tokens.shape
    span = attn_gain.shape[0]
    taps = conv_query.shape[0]
    heads = w_beta.shape[1]
    size = head_gain.shape[0] * devices
    ff = w_ffgate.shape[1]
    cols = width // team
    own_heads = heads // team
    ff_rows = w_ffdown.shape[0]
    member = lax.axis_index(TEAM)
    first = ff_rows * groups // 2 // 128 * 128
    first = (first + 128 if first * 2 < ff_rows * groups else first) // groups
    ff_parts = [(0, first), (first, ff_rows)]

    mixer_w = jnp.concatenate(
        [w.reshape(span, team, cols) for w in (w_query, w_key, w_value, w_gate)], axis=2
    ).transpose(1, 0, 2)
    mixer_sent = team_exchange(mixer_w).reshape(team * span, 4 * cols)
    mixer_all = group_gather(
        jnp.concatenate([mixer_sent, w_out.reshape(-1, 4 * cols)], axis=0)
    )

    small = jnp.concatenate(
        [
            attn_gain, mlp_gain,
            conv_query.reshape(-1), conv_key.reshape(-1), conv_value.reshape(-1),
            head_gain, w_beta.reshape(-1),
            group_ids.astype(BF), seq_weights.astype(BF),
        ]
    )
    small = jnp.pad(small, (0, -small.shape[0] % 128))
    small = gather_small(after(small, mixer_sent), groups)

    x_own = tokens.reshape(length, width)
    x_pieces = team_pieces(near_pieces(after(x_own, mixer_sent)))
    at = 0

    def take(count):
        nonlocal at
        part = small[:, at : at + count]
        at += count
        return part

    gain_one = take(span).reshape(-1).astype(F32)
    gain_two = take(span).reshape(-1).astype(F32)
    all_taps = [
        take(taps * span).reshape(devices, taps, span).transpose(1, 0, 2).reshape(taps, width)
        for _ in range(3)
    ]
    gain_head = take(head_gain.shape[0]).reshape(-1).astype(F32)
    beta_w = take(span * heads).reshape(width, heads)
    ids = take(1).reshape(-1)
    own_taps = lax.dynamic_slice_in_dim(
        jnp.concatenate(all_taps, axis=0).astype(F32), member * cols, cols, 1
    )
    own_taps = jnp.pad(own_taps, ((0, 16 - 3 * taps), (0, 0)))
    head_rows = jnp.pad(gain_head[None], ((0, 7), (0, 0)))
    beta_w = jnp.pad(
        lax.dynamic_slice_in_dim(beta_w, member * own_heads, own_heads, 1),
        ((0, 0), (0, 128 - own_heads)),
    )
    count = jnp.sum((ids.astype(F32) == group_ids.astype(F32)[0]).astype(jnp.int32)) * length
    factor = (
        seq_weights.astype(F32)[0] * (devices * seqs * length) / (GROUPS * count.astype(F32))
    )

    ff_own = []
    gates = [w.reshape(span, groups, team, ff_rows) for w in (w_ffgate, w_ffup)]
    sent = (small, x_pieces[6])
    for low, high in ff_parts:
        part = (high - low) * groups
        main = part // 128 * 128
        own = [
            w[..., low:high].transpose(2, 0, 1, 3).reshape(team, span, part) for w in gates
        ]
        own = [w[..., :main] for w in own] + [w[..., main:] for w in own]
        own = after(jnp.concatenate(own, axis=2), *sent)
        own = team_exchange(own).reshape(team * span, 2 * part)
        sent = (own,)
        ff_own.append(own)
    d_final = cotangent.reshape(length, width).astype(F32) * factor
    d_near = near_pieces(after(d_final.astype(BF), x_pieces[6]))
    x_pieces, d_near, ff_own = after((x_pieces, d_near, ff_own))
    ff_gu = [group_gather(ff_own[0])]
    down_w = group_gather(after(w_ffdown, ff_own[0]))
    ff_gu.append(group_gather(ff_own[1]))
    ff_gu = [v.reshape(width, -1) for v in ff_gu]
    ff_down = [down_w[:, low:high].reshape(-1, width) for low, high in ff_parts]

    gain_rows = jnp.pad(gain_one[None], ((0, 7), (0, 0)))
    normed, pre, beta_pre = project(x_pieces, gain_rows, mixer_all, beta_w)
    place = member.astype(jnp.int32).reshape(1)
    out_near = near_pieces(mixer_all[:, team * span :].reshape(groups * span, width))
    pre, out_near = after((pre, out_near))
    gated, inverse = delta_forward(
        place, pre, beta_pre, own_taps, head_rows, team, own_heads, size
    )
    d_down = team_pieces(after(d_near, out_near))
    gated, d_down[6], out_far = after((gated, d_down[6], far_piece(out_near)))
    gated, out_near, out_far = after((team_exchange(gated), out_near, out_far))
    out_pieces = [v.reshape(groups, span, width) for v in team_pieces(out_near, out_far)]
    gated = gated.transpose(1, 0, 2).reshape(length, width)
    out_full = assemble(place, out_pieces).reshape(width, width)
    inputs = x_own.astype(F32)
    resid = inputs + matmul(gated, out_full)

    unit_two, scale_two = rms_unit(resid)
    normed_two = team_pieces(near_pieces((unit_two * gain_two).astype(BF)))
    normed_two, d_down, hidden, d_gu, *sums = feed_forward(
        ff_gu[0], ff_down[0], normed_two, d_down
    )
    grad_gu = weight_grad(normed_two, d_gu).astype(BF)
    hidden_more, d_gu_more, dn_even, dn_odd, out_even, out_odd = feed_forward(
        ff_gu[1], ff_down[1], more=(normed_two, d_down) + tuple(after(sums, grad_gu))
    )
    ff_grads = [group_scatter(grad_gu)]
    terms = team_terms(dn_even, dn_odd)
    hidden, hidden_more = after((hidden, hidden_more), *terms)
    grad_gu = weight_grad(normed_two, d_gu_more).astype(BF)
    ff_grads.append(group_scatter(grad_gu))
    grad_down = jnp.concatenate(
        [
            weight_grad(v, d_down).astype(BF).reshape(groups, -1, width)
            for v in after((hidden, hidden_more), grad_gu)
        ],
        axis=1,
    )
    final_terms = team_terms(*after((out_even, out_odd), *terms))
    started = team_start(terms)
    started, grad_down, ff_grads[0] = after((started, grad_down, ff_grads[0]))
    grad_ffdown = group_scatter(grad_down.reshape(-1, width)).astype(F32)
    d_normed_two = team_end(started)
    gu_home_first = team_exchange(after(ff_grads[0], d_normed_two))
    mlp_part = jnp.sum(d_normed_two * unit_two, axis=0)
    d_resid = d_final + rms_pull(unit_two, scale_two, gain_two, d_normed_two)

    d_branch = d_resid.astype(BF)
    d_gated = back_grad(d_branch, out_full).astype(BF)
    d_gated_sent = d_gated.reshape(length, team, cols).transpose(1, 0, 2)
    d_gated_sent, gu_home_first = after((d_gated_sent, gu_home_first))
    d_gated = team_exchange(d_gated_sent)
    final_started = team_start(final_terms, d_gated)
    gated_rows = gated.reshape(length, groups, team, span)
    gated_rows = [
        lax.dynamic_index_in_dim(gated_rows, jnp.bitwise_xor(member, i), 2, False).reshape(
            length, groups * span
        )
        for i in range(team)
    ]
    out_terms = team_terms(
        *[
            weight_grad(jnp.concatenate(gated_rows[i::2], axis=1), d_branch).astype(BF)
            for i in range(2)
        ]
    )
    d_pre, d_beta, d_taps, d_head = delta_backward(
        place, pre, beta_pre, own_taps, head_rows, inverse, after(d_gated, *out_terms), team,
        own_heads, size
    )
    d_pre, final_started = after((d_pre, final_started))
    final_sum = team_end(final_started)
    grads = weight_grad(normed, d_pre).astype(BF)
    mixer_grads = group_scatter(grads)
    d_pre, grads, final_sum, ff_grads[1], grad_ffdown = after(
        (d_pre, grads, final_sum, ff_grads[1], grad_ffdown)
    )
    out_started = team_start(out_terms, final_sum)
    grad_beta = weight_grad(normed, d_beta)[:, :own_heads]
    dn_even, dn_odd, attn_part = pull_projections(
        d_pre, d_beta, x_pieces, mixer_all, beta_w
    )
    dn_even, dn_odd, out_started = after((dn_even, dn_odd, out_started))
    grad_out = team_end(out_started)
    in_terms = team_terms(dn_even, dn_odd)
    mixed = (resid + final_sum).astype(BF).reshape(seqs, length, width)
    gu_home = [gu_home_first, team_exchange(after(ff_grads[1], out_started))]
    in_terms, gu_home = after((in_terms, gu_home))
    in_started = team_start(in_terms)
    in_started, mixer_grads, grad_out = after((in_started, mixer_grads, grad_out))

    grad_out_home = group_sum_small(grad_out.reshape(groups, span, width), groups)

    ff_home = [[], []]
    for gu, (low, high) in zip(gu_home, ff_parts):
        part = (high - low) * groups
        main = part // 128 * 128
        gu = after(gu, mixer_grads).reshape(team, span, 2 * part)
        gate = jnp.concatenate([gu[..., :main], gu[..., 2 * main : part + main]], axis=2)
        up = jnp.concatenate([gu[..., main : 2 * main], gu[..., part + main :]], axis=2)
        for home, v in zip(ff_home, (gate, up)):
            home.append(v.reshape(team, span, groups, high - low).transpose(1, 2, 0, 3))
    grad_ffgate, grad_ffup = [
        jnp.concatenate(home, axis=3).reshape(span, ff).astype(F32) for home in ff_home
    ]
    mixer_grads = team_exchange(mixer_grads)
    mixer_grads = mixer_grads.reshape(team, span, 4, cols).transpose(2, 1, 0, 3)
    mixer_grads = mixer_grads.reshape(4, span, width).astype(F32)

    tap_rows = lax.dynamic_update_slice_in_dim(
        jnp.zeros((3 * taps, width), F32), d_taps[: 3 * taps], member * cols, 1
    )
    head_part = jnp.pad(
        d_head[0].reshape(devices, -1), ((0, 0), (0, span - head_gain.shape[0]))
    )
    extra = jnp.concatenate(
        [
            grad_beta, jnp.sum(attn_part, axis=0)[:, None], tap_rows.T,
            head_part.reshape(-1)[:, None], mlp_part[:, None],
        ],
        axis=1,
    )
    kinds = extra.shape[1]
    extra = after(extra, *in_terms[1:])
    extra = extra.reshape(groups, team, span * kinds)
    extra = jnp.pad(extra, ((0, 0), (0, 0), (0, -extra.shape[2] % 128)))
    extra = team_exchange(group_sum_small(extra, groups))
    extra = extra[:, : span * kinds].reshape(team, span, kinds)
    grad_beta = extra[:, :, :own_heads].transpose(1, 0, 2).reshape(span, heads)
    rest = jnp.sum(extra[:, :, own_heads:], axis=0)
    grad_attn = rest[:, 0]
    grad_taps = rest[:, 1 : 1 + 3 * taps].T.reshape(3, taps, span)
    grad_head = rest[: head_gain.shape[0], 1 + 3 * taps]
    grad_mlp = rest[:, 2 + 3 * taps]

    d_normed = team_end(in_started)
    unit_one, scale_one = rms_unit(inputs)
    input_grad = d_resid + rms_pull(unit_one, scale_one, gain_one, d_normed)
    return (
        mixed,
        input_grad.reshape(seqs, length, width),
        grad_attn,
        mixer_grads[0],
        mixer_grads[1],
        mixer_grads[2],
        mixer_grads[3],
        grad_beta,
        grad_taps[0],
        grad_taps[1],
        grad_taps[2],
        grad_head,
        grad_out_home,
        grad_mlp,
        grad_ffgate,
        grad_ffup,
        grad_ffdown,
    )


def solution(mesh):
    dp, fsdp = mesh.shape["dp"], mesh.shape["fsdp"]
    finer = jax.sharding.Mesh(mesh.devices.reshape(dp // 2, 2, fsdp // 2, 2), AXES)
    one, rows, last = P(AXES), P(AXES, None), P(None, AXES)
    seq = P(AXES, None, None)
    return jax.shard_map(
        on_device,
        mesh=finer,
        in_specs=(
            seq, one, one, seq, one, rows, rows, rows, rows, rows, last, last, last, one, rows,
            one, rows, rows, rows,
        ),
        out_specs=(
            seq, seq, one, rows, rows, rows, rows, rows, last, last, last, one, rows, one, rows,
            rows, rows,
        ),
        check_vma=False,
    )
```

```python
import collections
import functools
import jax
import jax.numpy as jnp
from jax import lax
from jax.experimental import pallas as pl
from jax.experimental.pallas import tpu as pltpu
from jax.sharding import PartitionSpec as P

EPS = 1e-06
BF = jnp.bfloat16
F32 = jnp.float32


def mm(left, right, dims):
    return lax.dot_general(left, right, ((dims[0], dims[1]), ((), ())), preferred_element_type=F32)


NN = ((1,), (0,))
NT = ((1,), (1,))
TN = ((0,), (0,))


def halves(value):
    high = value.astype(BF)
    return high, (value - high.astype(F32)).astype(BF)


def mm3(left, right, dims):
    lh, ll = left
    rh, rl = right
    return mm(lh, rh, dims) + (mm(lh, rl, dims) + mm(ll, rh, dims))


def mm2(left, right, dims):
    lh, ll = left
    return mm(lh, right, dims) + mm(ll, right, dims)


def sigmoid(v):
    return 1.0 / (1.0 + jnp.exp(-v))


def shift_down(v, count, rows):
    if count == 0:
        return v
    return jnp.where(rows >= count, pltpu.roll(v, count, 0), 0.0)


def shift_up(v, count, rows):
    if count == 0:
        return v
    length = v.shape[0]
    return jnp.where(rows < length - count, pltpu.roll(v, length - count, 0), 0.0)


def conv_of(pre, taps, rows):
    total = taps[0] * pre
    for j in range(1, len(taps)):
        total = total + taps[j] * shift_down(pre, j, rows)
    return total


def unit_inverses(stricts):
    size = stricts[0].shape[0]
    ri = lax.broadcasted_iota(jnp.int32, (size, size), 0)
    ci = lax.broadcasted_iota(jnp.int32, (size, size), 1)
    diff = jnp.bitwise_xor(ri, ci)
    eye = jnp.where(ri == ci, 1.0, 0.0)
    results = [eye - jnp.where(diff == 1, strict, 0.0) for strict in stricts]
    span = 2
    while span < size:
        here = (diff >= span) & (diff < 2 * span)
        split = [halves(result) for result in results]
        inner = [mm3(halves(jnp.where(here, s, 0.0)), r, NN) for s, r in zip(stricts, split)]
        inner = [halves(i) for i in inner]
        results = [t - mm3(r, i, NN) for t, r, i in zip(results, split, inner)]
        span *= 2
    return results


def head_forward(pre_q, pre_k, pre_v, beta_pre, taps):
    length, size = pre_q.shape
    rows = lax.broadcasted_iota(jnp.int32, (length, size), 0)
    cq = conv_of(pre_q, taps[0:4], rows)
    ck = conv_of(pre_k, taps[4:8], rows)
    cv = conv_of(pre_v, taps[8:12], rows)
    sq, sk, sv = sigmoid(cq), sigmoid(ck), sigmoid(cv)
    yq, yk, yv = cq * sq, ck * sk, cv * sv
    rq = lax.rsqrt(jnp.sum(yq * yq, axis=-1, keepdims=True) + EPS)
    rk = lax.rsqrt(jnp.sum(yk * yk, axis=-1, keepdims=True) + EPS)
    query = (yq * rq * size ** (-0.5)).astype(BF)
    key = (yk * rk).astype(BF)
    value = yv.astype(BF)
    beta = sigmoid(beta_pre)
    return (cq, ck, cv, sq, sk, sv, yq, yk, rq, rk, query, key, value, beta, rows)


def lower_masks(length):
    ri = lax.broadcasted_iota(jnp.int32, (length, length), 0)
    ci = lax.broadcasted_iota(jnp.int32, (length, length), 1)
    return ri > ci, ri >= ci


def fwd_kernel(
    place_ref, pre_ref, bpre_ref, taps_ref, gain_ref, gated_ref, inv_ref, *, heads, size, length
):
    half = length // 2
    width = heads * size
    flip = place_ref[0] & (gated_ref.shape[0] - 1)
    strictly, inclusive = lower_masks(length)
    work = []
    blocks = []
    chains = [(b, h) for b in range(pre_ref.shape[0] // length) for h in range(heads)]
    for b, h in chains:
        at = pl.ds(h * size, size)
        rows = pl.ds(b * length, length)
        pre = [pre_ref[rows, pl.ds(i * width + h * size, size)] for i in range(3)]
        taps = [taps_ref[i : i + 1, at] for i in range(12)]
        made = head_forward(*pre, bpre_ref[rows, h : h + 1], taps)
        query, key, value, beta = made[10:14]
        strict = jnp.where(strictly, mm(key, key, NT) * beta, 0.0)
        blocks += [strict[:half, :half], strict[half:, half:]]
        scores = jnp.where(inclusive, mm(query, key, NT), 0.0)
        work.append((halves(strict[half:, :half]), value.astype(F32) * beta, halves(scores)))
    inverses = unit_inverses(blocks)
    for n, (b, h) in enumerate(chains):
        inv_ref[b, h, 0] = inverses[2 * n]
        inv_ref[b, h, 1] = inverses[2 * n + 1]
    tops = [mm3(halves(inverses[2 * n]), halves(w[1][:half]), NN) for n, w in enumerate(work)]
    lows = [w[1][half:] - mm3(w[0], halves(top), NN) for w, top in zip(work, tops)]
    lows = [mm3(halves(inverses[2 * n + 1]), halves(low), NN) for n, low in enumerate(lows)]
    mixers = [
        mm3(w[2], halves(jnp.concatenate([top, low], axis=0)), NN)
        for w, top, low in zip(work, tops, lows)
    ]
    for (b, h), mixer in zip(chains, mixers):
        at = pl.ds(h * size, size)
        rows = pl.ds(b * length, length)
        scale = lax.rsqrt(jnp.mean(mixer * mixer, axis=-1, keepdims=True) + EPS)
        gate = pre_ref[rows, pl.ds(3 * width + h * size, size)]
        gated = mixer * scale * gain_ref[0:1, :] * (gate * sigmoid(gate))
        gated_ref[b ^ flip, :, at] = gated.astype(BF)


def bwd_chain(refs, b, h, heads, size, length, masks, sums):
    pre_ref, bpre_ref, taps_ref, gain_ref, inv_ref, dgated_ref, dpre_ref, dbeta_ref, flip = refs
    strictly, inclusive = masks
    half = length // 2
    width = heads * size
    at = pl.ds(h * size, size)
    line = pl.ds(b * length, length)
    cols = [pl.ds(i * width + h * size, size) for i in range(4)]
    taps = [taps_ref[i : i + 1, at] for i in range(12)]
    made = head_forward(
        *[pre_ref[line, c] for c in cols[:3]], bpre_ref[line, h : h + 1], taps
    )
    (cq, ck, cv, sq, sk, sv, yq, yk, rq, rk, query, key, value, beta, rows) = made
    yield
    gram = mm(key, key, NT)
    cross = halves((gram * beta)[half:, :half])
    scores = halves(jnp.where(inclusive, mm(query, key, NT), 0.0))
    top, low = halves(inv_ref[b, h, 0]), halves(inv_ref[b, h, 1])
    val = value.astype(F32)
    rhs = val * beta
    yield
    fresh_top = mm3(top, halves(rhs[:half]), NN)
    yield
    fresh_low = rhs[half:] - mm3(cross, halves(fresh_top), NN)
    yield
    fresh_low = mm3(low, halves(fresh_low), NN)
    fresh = halves(jnp.concatenate([fresh_top, fresh_low], axis=0))
    yield
    mixer = mm3(scores, fresh, NN)
    yield
    scale = lax.rsqrt(jnp.mean(mixer * mixer, axis=-1, keepdims=True) + EPS)
    gate = pre_ref[line, cols[3]]
    sg = sigmoid(gate)
    dgated = dgated_ref[b ^ flip, :, at].astype(F32)
    unit = mixer * scale
    gain = gain_ref[0:1, :]
    dgate = dgated * unit * gain * (sg * (1.0 + gate * (1.0 - sg)))
    dnorm = dgated * (gate * sg)
    sums["gain"].append(jnp.sum(dnorm * unit, axis=0, keepdims=True))
    dunit = dnorm * gain
    dmixer = scale * (dunit - unit * jnp.mean(dunit * unit, axis=-1, keepdims=True))
    dm = halves(dmixer)
    dpre_ref[line, cols[3]] = dgate.astype(BF)
    yield
    dscores = halves(jnp.where(inclusive, mm3(dm, fresh, NT), 0.0))
    dfresh = mm3(scores, dm, TN)
    yield
    drhs_low = mm3(low, halves(dfresh[half:]), TN)
    yield
    drhs_top = dfresh[:half] - mm3(cross, halves(drhs_low), TN)
    yield
    drhs_top = mm3(top, halves(drhs_top), TN)
    drhs = jnp.concatenate([drhs_top, drhs_low], axis=0)
    yield
    dstrict = jnp.where(strictly, -mm3(halves(drhs), fresh, NT), 0.0)
    dgram = halves(dstrict * beta)
    dval = drhs * beta
    dbeta = jnp.sum(dstrict * gram, axis=-1, keepdims=True) + jnp.sum(
        drhs * val, axis=-1, keepdims=True
    )
    dbeta_ref[line, h : h + 1] = (dbeta * beta * (1.0 - beta)).astype(BF)
    yield
    dquery = mm2(dscores, key, NN)
    dkey = mm2(dscores, query, TN) + mm2(dgram, key, NN) + mm2(dgram, key, TN)
    yield
    sc = size ** (-0.5)
    uq, uk = yq * rq, yk * rk
    dyq = (rq * sc) * (dquery - uq * jnp.sum(dquery * uq, axis=-1, keepdims=True))
    dyk = rk * (dkey - uk * jnp.sum(dkey * uk, axis=-1, keepdims=True))
    for i, (dy, s, c) in enumerate(((dyq, sq, cq), (dyk, sk, ck), (dval, sv, cv))):
        dc = dy * (s * (1.0 + c * (1.0 - s)))
        total = taps[4 * i] * dc
        for j in range(4):
            moved = shift_down(pre_ref[line, cols[i]], j, rows)
            sums[4 * i + j, h].append(jnp.sum(dc * moved, axis=0, keepdims=True))
            if j:
                total = total + taps[4 * i + j] * shift_up(dc, j, rows)
        dpre_ref[line, cols[i]] = total.astype(BF)
        yield


def bwd_kernel(
    place_ref, pre_ref, bpre_ref, taps_ref, gain_ref, inv_ref, dgated_ref,
    dpre_ref, dbeta_ref, dtaps_ref, dgain_ref, *, heads, size, length,
):
    @pl.when(pl.program_id(0) == 0)
    def _():
        dtaps_ref[...] = jnp.zeros_like(dtaps_ref)
        dgain_ref[...] = jnp.zeros_like(dgain_ref)

    dbeta_ref[...] = jnp.zeros_like(dbeta_ref)
    masks = lower_masks(length)
    sums = collections.defaultdict(list)
    flip = place_ref[0] & (dgated_ref.shape[0] - 1)
    refs = (
        pre_ref, bpre_ref, taps_ref, gain_ref, inv_ref, dgated_ref, dpre_ref, dbeta_ref, flip
    )
    chains = [
        bwd_chain(refs, b, h, heads, size, length, masks, sums)
        for b in range(dgated_ref.shape[0])
        for h in range(heads)
    ]
    while chains:
        chains = [chain for chain in chains if next(chain, True) is None]
    dgain_ref[0:1, :] += sum(sums.pop("gain"))
    for (row, h), parts in sums.items():
        dtaps_ref[row : row + 1, pl.ds(h * size, size)] += sum(parts)


PAIR = 2


def team_block(i, p):
    return (jnp.bitwise_xor(p[0] // PAIR, i), 0, 0)


def delta_forward(place, pre, bpre, taps, gain, slots, heads, size):
    rows = pre.shape[0]
    length = rows // slots
    width = heads * size
    return pl.pallas_call(
        functools.partial(fwd_kernel, heads=heads, size=size, length=length),
        grid_spec=pltpu.PrefetchScalarGridSpec(
            num_scalar_prefetch=1,
            grid=(slots // PAIR,),
            in_specs=[
                pl.BlockSpec((PAIR * length, 4 * width), lambda i, p: (i, 0)),
                pl.BlockSpec((PAIR * length, 128), lambda i, p: (i, 0)),
                pl.BlockSpec((16, width), lambda i, p: (0, 0)),
                pl.BlockSpec((8, size), lambda i, p: (0, 0)),
            ],
            out_specs=[
                pl.BlockSpec((PAIR, length, width), team_block),
                pl.BlockSpec((PAIR, heads, 2, length // 2, length // 2), lambda i, p: (i, 0, 0, 0, 0)),
            ],
        ),
        out_shape=[
            jax.ShapeDtypeStruct((slots, length, width), BF),
            jax.ShapeDtypeStruct((slots, heads, 2, length // 2, length // 2), F32),
        ],
        compiler_params=pltpu.CompilerParams(vmem_limit_bytes=48 * 1024 * 1024),
        cost_estimate=pl.CostEstimate(
            flops=slots * heads * 100_000_000, bytes_accessed=rows * width * 4, transcendentals=0
        ),
        name="delta_forward",
    )(place, pre, bpre, taps, gain)


def delta_backward(place, pre, bpre, taps, gain, inverse, dgated, slots, heads, size):
    rows = pre.shape[0]
    length = rows // slots
    width = heads * size
    return pl.pallas_call(
        functools.partial(bwd_kernel, heads=heads, size=size, length=length),
        grid_spec=pltpu.PrefetchScalarGridSpec(
            num_scalar_prefetch=1,
            grid=(slots // PAIR,),
            in_specs=[
                pl.BlockSpec((PAIR * length, 4 * width), lambda i, p: (i, 0)),
                pl.BlockSpec((PAIR * length, 128), lambda i, p: (i, 0)),
                pl.BlockSpec((16, width), lambda i, p: (0, 0)),
                pl.BlockSpec((8, size), lambda i, p: (0, 0)),
                pl.BlockSpec((PAIR, heads, 2, length // 2, length // 2), lambda i, p: (i, 0, 0, 0, 0)),
                pl.BlockSpec((PAIR, length, width), team_block),
            ],
            out_specs=[
                pl.BlockSpec((PAIR * length, 4 * width), lambda i, p: (i, 0)),
                pl.BlockSpec((PAIR * length, 128), lambda i, p: (i, 0)),
                pl.BlockSpec((16, width), lambda i, p: (0, 0)),
                pl.BlockSpec((8, size), lambda i, p: (0, 0)),
            ],
        ),
        out_shape=[
            jax.ShapeDtypeStruct((rows, 4 * width), BF),
            jax.ShapeDtypeStruct((rows, 128), BF),
            jax.ShapeDtypeStruct((16, width), F32),
            jax.ShapeDtypeStruct((8, size), F32),
        ],
        compiler_params=pltpu.CompilerParams(vmem_limit_bytes=48 * 1024 * 1024),
        cost_estimate=pl.CostEstimate(
            flops=slots * heads * 100_000_000, bytes_accessed=rows * width * 4, transcendentals=0
        ),
        name="delta_backward",
    )(place, pre, bpre, taps, gain, inverse, dgated)


def load_piece(step, pieces, buf, sem):
    def start(which):
        for n, piece in enumerate(pieces):

            @pl.when(which == n)
            def _():
                pltpu.make_async_copy(piece, buf.at[n % 2], sem.at[n % 2]).start()

    @pl.when(step == 0)
    def _():
        start(0)

    start(step + 1)
    slot = lax.rem(step, 2)
    pltpu.make_async_copy(pieces[0], buf.at[slot], sem.at[slot]).wait()
    return buf[slot]


def piece_scratch(piece):
    return [pltpu.VMEM((2,) + piece.shape, piece.dtype), pltpu.SemaphoreType.DMA((2,))]


ANY = pl.BlockSpec(memory_space=pl.ANY)


def assemble_kernel(place_ref, *refs):
    *pieces, out_ref, buf, sem = refs
    out_ref[:, 0] = load_piece(pl.program_id(0), pieces, buf, sem)


def assemble(place, pieces):
    groups, rows, width = pieces[0].shape
    count = len(pieces)
    return pl.pallas_call(
        assemble_kernel,
        grid_spec=pltpu.PrefetchScalarGridSpec(
            num_scalar_prefetch=1,
            grid=(count,),
            in_specs=[ANY] * count,
            out_specs=pl.BlockSpec(
                (groups, 1, rows, width), lambda i, p: (0, jnp.bitwise_xor(p[0], i), 0, 0)
            ),
            scratch_shapes=piece_scratch(pieces[0]),
        ),
        out_shape=jax.ShapeDtypeStruct((groups, count, rows, width), BF),
        cost_estimate=pl.CostEstimate(
            flops=0, bytes_accessed=4 * count * groups * rows * width, transcendentals=0
        ),
        name="assemble",
    )(place, *pieces)


def ff_tile(n, d, gu_ref, down_ref, hid_ref, dgu_ref):
    cols = hid_ref.shape[1]
    main = cols // 128 * 128
    gu_w = gu_ref[...]
    gu = mm(n, gu_w, NN)
    dh = mm(d, down_ref[...], NT)
    spans = [(0, main, main, 0)]
    if main < cols:
        spans.append((2 * main, main + cols, cols - main, main))
    for gate_at, up_at, count, at in spans:
        gate, up = gu[:, gate_at : gate_at + count], gu[:, up_at : up_at + count]
        grad = dh[:, at : at + count]
        sig = sigmoid(gate)
        silu = gate * sig
        hid_ref[:, at : at + count] = (silu * up).astype(BF)
        dgu_ref[:, gate_at : gate_at + count] = (grad * up * (sig + silu * (1.0 - sig))).astype(BF)
        dgu_ref[:, up_at : up_at + count] = (grad * silu).astype(BF)
    return mm(dgu_ref[...], gu_w, NT), mm(hid_ref[...], down_ref[...], NN)


def ff_first_kernel(gu_ref, down_ref, *refs):
    ns, ds = refs[:8], refs[8:16]
    n_ref, d_ref, hid_ref, dgu_ref, dn_ref, out_ref, n_buf, n_sem, d_buf, d_sem = refs[16:]
    step = pl.program_id(0)
    n = load_piece(step, ns, n_buf, n_sem)
    d = load_piece(step, ds, d_buf, d_sem)
    n_ref[...] = n
    d_ref[...] = d
    dn, out = ff_tile(n, d, gu_ref, down_ref, hid_ref, dgu_ref)
    dn_ref[...] = dn.astype(BF)
    out_ref[...] = out.astype(BF)


def put_pair(step, value, even_ref, odd_ref):
    value = value.astype(BF)

    @pl.when(lax.rem(step, 2) == 0)
    def _():
        even_ref[...] = value

    @pl.when(lax.rem(step, 2) == 1)
    def _():
        odd_ref[...] = value


def ff_more_kernel(
    gu_ref, down_ref, n_ref, d_ref, dn_in, out_in,
    hid_ref, dgu_ref, dn_even, dn_odd, out_even, out_odd,
):
    dn, out = ff_tile(n_ref[...], d_ref[...], gu_ref, down_ref, hid_ref, dgu_ref)
    step = pl.program_id(0)
    put_pair(step, dn + dn_in[...].astype(F32), dn_even, dn_odd)
    put_pair(step, out + out_in[...].astype(F32), out_even, out_odd)


def feed_forward(gu, down, ns=None, ds=None, more=None):
    cols, width = down.shape
    tile = ns[0].shape[0] if more is None else more[0].shape[0] // 8
    rows = 8 * tile

    def row(count):
        return pl.BlockSpec((tile, count), lambda i: (i, 0))

    pair = pl.BlockSpec((tile, width), lambda i: (i // 2, 0))
    if more is None:
        outs = [width, width, cols, 2 * cols, width, width]
        out_specs = [row(k) for k in outs]
        shapes = [(rows, k) for k in outs]
    else:
        out_specs = [row(cols), row(2 * cols)] + [pair] * 4
        shapes = [(rows, cols), (rows, 2 * cols)] + [(rows // 2, width)] * 4
    return pl.pallas_call(
        ff_first_kernel if more is None else ff_more_kernel,
        grid=(8,),
        in_specs=[
            pl.BlockSpec((width, 2 * cols), lambda i: (0, 0)),
            pl.BlockSpec((cols, width), lambda i: (0, 0)),
        ]
        + ([ANY] * 16 if more is None else [row(width)] * 4),
        out_specs=out_specs,
        out_shape=[jax.ShapeDtypeStruct(k, BF) for k in shapes],
        scratch_shapes=piece_scratch(ns[0]) + piece_scratch(ds[0]) if more is None else [],
        compiler_params=pltpu.CompilerParams(vmem_limit_bytes=56 * 1024 * 1024),
        cost_estimate=pl.CostEstimate(
            flops=rows * width * cols, bytes_accessed=2 * rows * width, transcendentals=0
        ),
        name="feed_forward",
    )(gu, down, *(tuple(ns) + tuple(ds) if more is None else more))


def pull_kernel(dpre_ref, dbeta_ref, w_ref, beta_ref, *refs):
    even_ref, odd_ref, part_ref, buf, sem = refs[8:]

    @pl.when(pl.program_id(0) == 0)
    def _():
        part_ref[...] = jnp.zeros_like(part_ref)

    x = load_piece(pl.program_id(0), refs[:8], buf, sem).astype(F32)
    unit = x * lax.rsqrt(jnp.mean(x * x, axis=-1, keepdims=True) + EPS)
    w = w_ref[...].reshape(-1, w_ref.shape[-1])
    dn = mm(dpre_ref[...], w, NT) + mm(dbeta_ref[...], beta_ref[...], NT)
    part_ref[...] += jnp.sum((dn * unit).reshape(-1, 8, dn.shape[1]), axis=0)
    put_pair(pl.program_id(0), dn, even_ref, odd_ref)


def pull_projections(dpre, dbeta, x, w, beta_w):
    tile, width = x[0].shape
    rows, cols = dpre.shape
    groups = w.shape[0]

    def row(count):
        return pl.BlockSpec((tile, count), lambda i: (i, 0))

    return pl.pallas_call(
        pull_kernel,
        grid=(rows // tile,),
        in_specs=[
            row(cols),
            row(dbeta.shape[1]),
            pl.BlockSpec((groups, width // groups, cols), lambda i: (0, 0, 0)),
            pl.BlockSpec(beta_w.shape, lambda i: (0, 0)),
        ]
        + [ANY] * 8,
        scratch_shapes=piece_scratch(x[0]),
        out_specs=[pl.BlockSpec((tile, width), lambda i: (i // 2, 0))] * 2
        + [pl.BlockSpec((8, width), lambda i: (0, 0))],
        out_shape=[
            jax.ShapeDtypeStruct((rows // 2, width), BF),
            jax.ShapeDtypeStruct((rows // 2, width), BF),
            jax.ShapeDtypeStruct((8, width), F32),
        ],
        compiler_params=pltpu.CompilerParams(vmem_limit_bytes=48 * 1024 * 1024),
        cost_estimate=pl.CostEstimate(
            flops=rows * width * cols // 4, bytes_accessed=rows * width, transcendentals=0
        ),
        name="pull_projections",
    )(dpre, dbeta, w, beta_w, *x)


def project_kernel(gain_ref, w_ref, beta_ref, *refs):
    n_ref, pre_ref, bpre_ref, buf, sem = refs[8:]
    x = load_piece(pl.program_id(0), refs[:8], buf, sem).astype(F32)
    unit = x * lax.rsqrt(jnp.mean(x * x, axis=-1, keepdims=True) + EPS)
    n = (unit * gain_ref[0:1, :]).astype(BF)
    n_ref[...] = n
    pre_ref[...] = mm(n, w_ref[...].reshape(-1, w_ref.shape[-1]), NN)
    bpre_ref[...] = mm(n, beta_ref[...], NN)


def project(x, gain, w, beta_w):
    tile, width = x[0].shape
    rows = 8 * tile
    groups, _, cols = w.shape

    def row(count):
        return pl.BlockSpec((tile, count), lambda i: (i, 0))

    return pl.pallas_call(
        project_kernel,
        grid=(rows // tile,),
        in_specs=[
            pl.BlockSpec((8, width), lambda i: (0, 0)),
            pl.BlockSpec((groups, width // groups, cols), lambda i: (0, 0, 0)),
            pl.BlockSpec(beta_w.shape, lambda i: (0, 0)),
        ]
        + [ANY] * 8,
        scratch_shapes=piece_scratch(x[0]),
        out_specs=[row(width), row(cols), row(beta_w.shape[1])],
        out_shape=[
            jax.ShapeDtypeStruct((rows, width), BF),
            jax.ShapeDtypeStruct((rows, cols), F32),
            jax.ShapeDtypeStruct((rows, beta_w.shape[1]), F32),
        ],
        compiler_params=pltpu.CompilerParams(vmem_limit_bytes=48 * 1024 * 1024),
        cost_estimate=pl.CostEstimate(
            flops=rows * width * cols // 4, bytes_accessed=rows * width, transcendentals=0
        ),
        name="project",
    )(gain, w, beta_w, *x)


GROUPS = 8
AXES = ("g", "a", "b", "c")
TEAM = ("a", "b", "c")
SWAP = ((0, 1), (1, 0))
CROSS = ((0, 3), (1, 2), (2, 1), (3, 0))


def swap_a(v):
    return lax.ppermute(v, "a", SWAP)


def swap_b(v):
    return lax.ppermute(v, "b", SWAP)


def swap_c(v):
    return lax.ppermute(v, "c", SWAP)


def after(v, *others):
    if not others:
        return lax.optimization_barrier(v)
    return lax.optimization_barrier((v,) + others)[0]


def plus(left, right):
    return (left.astype(F32) + right.astype(F32)).astype(BF)


def near_pieces(v):
    return v, swap_b(v), swap_a(v)


def far_piece(near):
    _, from_b, from_a = near
    rows = from_a.shape[0] // 2
    return jnp.concatenate([swap_b(from_a[:rows]), swap_a(from_b[rows:])], axis=0)


def team_pieces(near, far=None):
    pieces = []
    for v in (*near, far_piece(near) if far is None else far):
        pieces += [v, swap_c(v)]
    return pieces


def team_terms(even, odd):
    length = even.shape[0] // 4
    got = swap_c(odd)
    parts = [[v[i * length : (i + 1) * length] for v in (even, got)] for i in range(4)]
    (mine, other), *rest = parts
    return [mine.astype(F32) + other.astype(F32)] + [plus(mine, other) for mine, other in rest]


def team_start(terms, *others):
    own, near_b, near_a, far = terms
    rows = far.shape[0] // 2
    near_b, near_a, far = after((near_b, near_a, far), *others)
    via_a, via_b = swap_a(far[:rows]), swap_b(far[rows:])
    from_a, from_b = swap_a(near_a[:rows]), swap_b(near_b[rows:])
    return own, near_b[:rows], near_a[rows:], via_a, via_b, from_a, from_b


def team_end(started, *others):
    own, near_b, near_a, via_a, via_b, from_a, from_b = started
    via_a, via_b = after((via_a, via_b), *others)
    late_a = swap_a(plus(near_a, via_b))
    late_b = swap_b(plus(near_b, via_a))
    sums = jnp.concatenate(
        [
            from_a.astype(F32) + late_b.astype(F32),
            late_a.astype(F32) + from_b.astype(F32),
        ],
        axis=0,
    )
    return own + sums


def team_exchange(v):
    return lax.all_to_all(v, TEAM, 0, 0, tiled=True)


def matmul(left, right):
    return jnp.dot(left, right, preferred_element_type=F32)


def weight_grad(left, right):
    return jnp.einsum("ra,rb->ab", left, right, preferred_element_type=F32)


def back_grad(grad, weight):
    return jnp.einsum("rb,ab->ra", grad, weight, preferred_element_type=F32)


def rms_unit(value):
    scale = lax.rsqrt(jnp.mean(value * value, axis=-1, keepdims=True) + EPS)
    return value * scale, scale


def rms_pull(unit, scale, gain, grad):
    inner = grad * gain
    return scale * (inner - unit * jnp.mean(inner * unit, axis=-1, keepdims=True))


def gather_small(v, groups):
    both = v[None]
    for axis, swap in (("c", swap_c), ("b", swap_b), ("a", swap_a)):
        other = swap(both)
        mine = lax.axis_index(axis) == 0
        both = jnp.concatenate(
            [jnp.where(mine, both, other), jnp.where(mine, other, both)], axis=0
        )
    me = lax.axis_index("g")
    whole = jnp.zeros((groups,) + both.shape, both.dtype)
    whole = lax.dynamic_update_index_in_dim(whole, both, me, 0)
    for step in range(1, groups):
        got = lax.ppermute(both, "g", [(j, (j + step) % groups) for j in range(groups)])
        whole = lax.dynamic_update_index_in_dim(whole, got, (me - step) % groups, 0)
    return whole.reshape(-1, v.shape[0])


def group_sum_small(v, groups):
    me = lax.axis_index("g")
    total = lax.dynamic_index_in_dim(v, me, 0, False)
    for step in range(1, groups):
        send = lax.dynamic_index_in_dim(v, (me + step) % groups, 0, False).astype(BF)
        got = lax.ppermute(send, "g", [(j, (j + step) % groups) for j in range(groups)])
        total = total + got.astype(F32)
    return total


def group_scatter(v):
    return lax.psum_scatter(v, "g", scatter_dimension=0, tiled=True)


def group_gather(v):
    return lax.all_gather(v, "g", axis=0, tiled=False)


def on_device(
    tokens, group_ids, seq_weights, cotangent, attn_gain, w_query, w_key, w_value, w_gate, w_beta,
    conv_query, conv_key, conv_value, head_gain, w_out, mlp_gain, w_ffgate, w_ffup, w_ffdown,
):
    groups = lax.axis_size("g")
    team = 8
    devices = groups * team
    seqs, length, width = tokens.shape
    span = attn_gain.shape[0]
    taps = conv_query.shape[0]
    heads = w_beta.shape[1]
    size = head_gain.shape[0] * devices
    ff = w_ffgate.shape[1]
    cols = width // team
    own_heads = heads // team
    ff_rows = w_ffdown.shape[0]
    member = lax.axis_index(TEAM)
    first = ff_rows * groups // 2 // 128 * 128
    first = (first + 128 if first * 2 < ff_rows * groups else first) // groups
    ff_parts = [(0, first), (first, ff_rows)]

    mixer_w = jnp.concatenate(
        [w.reshape(span, team, cols) for w in (w_query, w_key, w_value, w_gate)], axis=2
    ).transpose(1, 0, 2)
    mixer_sent = team_exchange(mixer_w).reshape(team * span, 4 * cols)
    mixer_all = group_gather(
        jnp.concatenate([mixer_sent, w_out.reshape(-1, 4 * cols)], axis=0)
    )

    small = jnp.concatenate(
        [
            attn_gain, mlp_gain,
            conv_query.reshape(-1), conv_key.reshape(-1), conv_value.reshape(-1),
            head_gain, w_beta.reshape(-1),
            group_ids.astype(BF), seq_weights.astype(BF),
        ]
    )
    small = jnp.pad(small, (0, -small.shape[0] % 128))
    small = gather_small(after(small, mixer_sent), groups)

    x_own = tokens.reshape(length, width)
    x_pieces = team_pieces(near_pieces(after(x_own, mixer_sent)))
    at = 0

    def take(count):
        nonlocal at
        part = small[:, at : at + count]
        at += count
        return part

    gain_one = take(span).reshape(-1).astype(F32)
    gain_two = take(span).reshape(-1).astype(F32)
    all_taps = [
        take(taps * span).reshape(devices, taps, span).transpose(1, 0, 2).reshape(taps, width)
        for _ in range(3)
    ]
    gain_head = take(head_gain.shape[0]).reshape(-1).astype(F32)
    beta_w = take(span * heads).reshape(width, heads)
    ids = take(1).reshape(-1)
    own_taps = lax.dynamic_slice_in_dim(
        jnp.concatenate(all_taps, axis=0).astype(F32), member * cols, cols, 1
    )
    own_taps = jnp.pad(own_taps, ((0, 16 - 3 * taps), (0, 0)))
    head_rows = jnp.pad(gain_head[None], ((0, 7), (0, 0)))
    beta_w = jnp.pad(
        lax.dynamic_slice_in_dim(beta_w, member * own_heads, own_heads, 1),
        ((0, 0), (0, 128 - own_heads)),
    )
    count = jnp.sum((ids.astype(F32) == group_ids.astype(F32)[0]).astype(jnp.int32)) * length
    factor = (
        seq_weights.astype(F32)[0] * (devices * seqs * length) / (GROUPS * count.astype(F32))
    )

    ff_own = []
    gates = [w.reshape(span, groups, team, ff_rows) for w in (w_ffgate, w_ffup)]
    sent = (small, x_pieces[6])
    for low, high in ff_parts:
        part = (high - low) * groups
        main = part // 128 * 128
        own = [
            w[..., low:high].transpose(2, 0, 1, 3).reshape(team, span, part) for w in gates
        ]
        own = [w[..., :main] for w in own] + [w[..., main:] for w in own]
        own = after(jnp.concatenate(own, axis=2), *sent)
        own = team_exchange(own).reshape(team * span, 2 * part)
        sent = (own,)
        ff_own.append(own)
    d_final = cotangent.reshape(length, width).astype(F32) * factor
    d_near = near_pieces(after(d_final.astype(BF), x_pieces[6]))
    x_pieces, d_near, ff_own = after((x_pieces, d_near, ff_own))
    ff_gu = [group_gather(ff_own[0])]
    down_w = group_gather(after(w_ffdown, ff_own[0]))
    ff_gu.append(group_gather(ff_own[1]))
    ff_gu = [v.reshape(width, -1) for v in ff_gu]
    ff_down = [down_w[:, low:high].reshape(-1, width) for low, high in ff_parts]

    gain_rows = jnp.pad(gain_one[None], ((0, 7), (0, 0)))
    normed, pre, beta_pre = project(x_pieces, gain_rows, mixer_all, beta_w)
    place = member.astype(jnp.int32).reshape(1)
    out_near = near_pieces(mixer_all[:, team * span :].reshape(groups * span, width))
    pre, out_near = after((pre, out_near))
    gated, inverse = delta_forward(
        place, pre, beta_pre, own_taps, head_rows, team, own_heads, size
    )
    d_down = team_pieces(after(d_near, out_near))
    gated, d_down[6], out_far = after((gated, d_down[6], far_piece(out_near)))
    gated, out_near, out_far = after((team_exchange(gated), out_near, out_far))
    out_pieces = [v.reshape(groups, span, width) for v in team_pieces(out_near, out_far)]
    gated = gated.transpose(1, 0, 2).reshape(length, width)
    out_full = assemble(place, out_pieces).reshape(width, width)
    inputs = x_own.astype(F32)
    resid = inputs + matmul(gated, out_full)

    unit_two, scale_two = rms_unit(resid)
    normed_two = team_pieces(near_pieces((unit_two * gain_two).astype(BF)))
    normed_two, d_down, hidden, d_gu, *sums = feed_forward(
        ff_gu[0], ff_down[0], normed_two, d_down
    )
    grad_gu = weight_grad(normed_two, d_gu).astype(BF)
    hidden_more, d_gu_more, dn_even, dn_odd, out_even, out_odd = feed_forward(
        ff_gu[1], ff_down[1], more=(normed_two, d_down) + tuple(after(sums, grad_gu))
    )
    ff_grads = [group_scatter(grad_gu)]
    terms = team_terms(dn_even, dn_odd)
    hidden, hidden_more = after((hidden, hidden_more), *terms)
    grad_gu = weight_grad(normed_two, d_gu_more).astype(BF)
    ff_grads.append(group_scatter(grad_gu))
    grad_down = jnp.concatenate(
        [
            weight_grad(v, d_down).astype(BF).reshape(groups, -1, width)
            for v in after((hidden, hidden_more), grad_gu)
        ],
        axis=1,
    )
    final_terms = team_terms(*after((out_even, out_odd), *terms))
    started = team_start(terms)
    started, grad_down, ff_grads[0] = after((started, grad_down, ff_grads[0]))
    grad_ffdown = group_scatter(grad_down.reshape(-1, width)).astype(F32)
    d_normed_two = team_end(started)
    gu_home_first = team_exchange(after(ff_grads[0], d_normed_two))
    mlp_part = jnp.sum(d_normed_two * unit_two, axis=0)
    d_resid = d_final + rms_pull(unit_two, scale_two, gain_two, d_normed_two)

    d_branch = d_resid.astype(BF)
    d_gated = back_grad(d_branch, out_full).astype(BF)
    d_gated_sent = d_gated.reshape(length, team, cols).transpose(1, 0, 2)
    d_gated_sent, gu_home_first = after((d_gated_sent, gu_home_first))
    d_gated = team_exchange(d_gated_sent)
    final_started = team_start(final_terms, d_gated)
    gated_rows = gated.reshape(length, groups, team, span)
    gated_rows = [
        lax.dynamic_index_in_dim(gated_rows, jnp.bitwise_xor(member, i), 2, False).reshape(
            length, groups * span
        )
        for i in range(team)
    ]
    out_terms = team_terms(
        *[
            weight_grad(jnp.concatenate(gated_rows[i::2], axis=1), d_branch).astype(BF)
            for i in range(2)
        ]
    )
    d_pre, d_beta, d_taps, d_head = delta_backward(
        place, pre, beta_pre, own_taps, head_rows, inverse, after(d_gated, *out_terms), team,
        own_heads, size
    )
    d_pre, final_started = after((d_pre, final_started))
    final_sum = team_end(final_started)
    grads = weight_grad(normed, d_pre).astype(BF)
    mixer_grads = group_scatter(grads)
    d_pre, grads, final_sum, ff_grads[1], grad_ffdown = after(
        (d_pre, grads, final_sum, ff_grads[1], grad_ffdown)
    )
    out_started = team_start(out_terms, final_sum)
    grad_beta = weight_grad(normed, d_beta)[:, :own_heads]
    dn_even, dn_odd, attn_part = pull_projections(
        d_pre, d_beta, x_pieces, mixer_all, beta_w
    )
    dn_even, dn_odd, out_started = after((dn_even, dn_odd, out_started))
    grad_out = team_end(out_started)
    in_terms = team_terms(dn_even, dn_odd)
    mixed = (resid + final_sum).astype(BF).reshape(seqs, length, width)
    gu_home = [gu_home_first, team_exchange(after(ff_grads[1], out_started))]
    in_terms, gu_home, mixer_grads = after((in_terms, gu_home, mixer_grads))
    in_started = team_start(in_terms)
    in_started, gu_home, grad_out = after((in_started, gu_home, grad_out))

    grad_out_home = group_sum_small(grad_out.reshape(groups, span, width), groups)

    ff_home = [[], []]
    for gu, (low, high) in zip(gu_home, ff_parts):
        part = (high - low) * groups
        main = part // 128 * 128
        gu = gu.reshape(team, span, 2 * part)
        gate = jnp.concatenate([gu[..., :main], gu[..., 2 * main : part + main]], axis=2)
        up = jnp.concatenate([gu[..., main : 2 * main], gu[..., part + main :]], axis=2)
        for home, v in zip(ff_home, (gate, up)):
            home.append(v.reshape(team, span, groups, high - low).transpose(1, 2, 0, 3))
    grad_ffgate, grad_ffup = [
        jnp.concatenate(home, axis=3).reshape(span, ff).astype(F32) for home in ff_home
    ]
    mixer_grads = team_exchange(mixer_grads)
    mixer_grads = mixer_grads.reshape(team, span, 4, cols).transpose(2, 1, 0, 3)
    mixer_grads = mixer_grads.reshape(4, span, width).astype(F32)

    tap_rows = lax.dynamic_update_slice_in_dim(
        jnp.zeros((3 * taps, width), F32), d_taps[: 3 * taps], member * cols, 1
    )
    head_part = jnp.pad(
        d_head[0].reshape(devices, -1), ((0, 0), (0, span - head_gain.shape[0]))
    )
    extra = jnp.concatenate(
        [
            grad_beta, jnp.sum(attn_part, axis=0)[:, None], tap_rows.T,
            head_part.reshape(-1)[:, None], mlp_part[:, None],
        ],
        axis=1,
    )
    kinds = extra.shape[1]
    extra = after(extra, *in_terms[1:])
    extra = extra.reshape(groups, team, span * kinds)
    extra = jnp.pad(extra, ((0, 0), (0, 0), (0, -extra.shape[2] % 128)))
    extra = team_exchange(group_sum_small(extra, groups))
    extra = extra[:, : span * kinds].reshape(team, span, kinds)
    grad_beta = extra[:, :, :own_heads].transpose(1, 0, 2).reshape(span, heads)
    rest = jnp.sum(extra[:, :, own_heads:], axis=0)
    grad_attn = rest[:, 0]
    grad_taps = rest[:, 1 : 1 + 3 * taps].T.reshape(3, taps, span)
    grad_head = rest[: head_gain.shape[0], 1 + 3 * taps]
    grad_mlp = rest[:, 2 + 3 * taps]

    d_normed = team_end(in_started)
    unit_one, scale_one = rms_unit(inputs)
    input_grad = d_resid + rms_pull(unit_one, scale_one, gain_one, d_normed)
    return (
        mixed,
        input_grad.reshape(seqs, length, width),
        grad_attn,
        mixer_grads[0],
        mixer_grads[1],
        mixer_grads[2],
        mixer_grads[3],
        grad_beta,
        grad_taps[0],
        grad_taps[1],
        grad_taps[2],
        grad_head,
        grad_out_home,
        grad_mlp,
        grad_ffgate,
        grad_ffup,
        grad_ffdown,
    )


def solution(mesh):
    dp, fsdp = mesh.shape["dp"], mesh.shape["fsdp"]
    finer = jax.sharding.Mesh(mesh.devices.reshape(dp // 2, 2, fsdp // 2, 2), AXES)
    one, rows, last = P(AXES), P(AXES, None), P(None, AXES)
    seq = P(AXES, None, None)
    return jax.shard_map(
        on_device,
        mesh=finer,
        in_specs=(
            seq, one, one, seq, one, rows, rows, rows, rows, rows, last, last, last, one, rows,
            one, rows, rows, rows,
        ),
        out_specs=(
            seq, seq, one, rows, rows, rows, rows, rows, last, last, last, one, rows, one, rows,
            rows, rows,
        ),
        check_vma=False,
    )
```
